512 devices in a mesh: slab: 64 (over z, y), patch: 8 (over x, core).
Axes of the slice: x: 4, y: 8, z: 8, core: 2. Of those that a mesh axis runs over, the one named last changes fastest.
Arguments:
- density: float32 [262144], P(('slab', 'patch')), may hold values from -6 to 6
- counts: int32 [512, 512], P(('slab', 'patch')), may hold values from 1 to 8, as said below
- send_panel: int32 [512, 512, 8], P(('slab', 'patch')), may hold values from 0 to 511
- send_weight: float32 [512, 512, 8], P(('slab', 'patch')), may hold values from -4 to 4
- interp_weight: float32 [512, 512, 8], P(('slab', 'patch')), may hold values from -4 to 4
- recv_row: int32 [512, 512, 8], P(('slab', 'patch')), may hold values from 0 to 255
- recv_col: int32 [512, 512, 8], P(('slab', 'patch')), may hold values from 0 to 511
- kernel: float32 [512, 512, 256], P(('slab', 'patch')), may hold values from 0.1 to 3, as said below
- near_index: int32 [16, 262144], P(None, ('slab', 'patch')), may hold values from 0 to 4095
- near_coef: float32 [16, 262144], P(None, ('slab', 'patch')), may hold values from -1 to 1
Outputs:
- potential: float32 [262144], P(('slab', 'patch'))
The draws below stay inside these ranges and needn't reach their ends.
Inputs may be any that keep to these rules, and one draw needn't show every extreme that they name: counts[a, b] is the number of used slots of the 8 from device a to grid owner b; in every draw some owner receives 8 from every device, and every device sends 8 to some owner. kernel[kx, ky, kz] = kernel[(-kx) mod 512, (-ky) mod 512, (-kz) mod 256].
All inputs are finite; a program needn't handle non-finite values.
Results may differ from the reference program's by a relative error of at most 0.00011.
Values sent between devices are 32-bit elements; how exact they have to be, the bound alone decides.
No kernel may reach another device: no remote copies, remote signals or barrier semaphores. Data moves between devices by JAX's collectives and lax.ppermute only.
A program may use at most 64 MiB of HBM per device.

```python
import jax
import jax.numpy as jnp

NX = 512
NY = 512
NZ = 256
P_DEV = 512
CAP = 8
NEAR = 16
PANELS = 262144
CELLS_DEV = 256
N_SLAB = 64
N_PATCH = 8
DEVICES = 512


def draw_counts(key, part):
    key = jax.random.fold_in(key, 11)
    keys = jax.random.split(key, 6)
    devices = N_SLAB * N_PATCH
    base = jax.random.randint(keys[0], (devices, devices), CAP // 8, CAP // 2 + 1)
    extra = jax.random.randint(keys[1], (devices, devices), CAP // 2, CAP + 1)
    heavy = jax.random.randint(keys[2], (N_SLAB,), 0, 8) == 0
    chosen = jax.random.randint(keys[3], (), 0, N_SLAB)
    heavy = heavy | (jnp.arange(N_SLAB, dtype=jnp.int32) == chosen)
    column = jnp.arange(devices, dtype=jnp.int32)
    heavy_col = heavy[column // N_PATCH]
    loads = jnp.where(heavy_col[None, :], extra, base)
    full_owner = jax.random.randint(keys[4], (), 0, devices)
    full_row = jax.random.randint(keys[5], (devices,), 0, devices)
    filled = (column[None, :] == full_owner) | (column[None, :] == full_row[:, None])
    return jnp.where(filled, CAP, loads).astype(jnp.int32)


def draw_kernel(key, part):
    key = jax.random.fold_in(key, 23)
    logs = jax.random.uniform(key, (NX, NY, NZ), jnp.float32, jnp.log(0.1), jnp.log(3.0))
    field = jnp.exp(logs)
    flip_x = -jnp.arange(NX, dtype=jnp.int32) % NX
    flip_y = -jnp.arange(NY, dtype=jnp.int32) % NY
    flip_z = -jnp.arange(NZ, dtype=jnp.int32) % NZ
    mirrored = field[flip_x][:, flip_y][:, :, flip_z]
    return jnp.clip(0.5 * (field + mirrored), 0.1, 3.0).astype(jnp.float32)


def place_ends(drawn, key, smallest, largest):
    longest = drawn.shape.index(max(drawn.shape))
    spots = []
    for shift in (0, 1):
        where = [jax.random.randint(jax.random.fold_in(key, axis), (), 0, length) for axis, length in enumerate(drawn.shape)]
        where[longest] = (where[longest] + shift) % drawn.shape[longest]
        spots.append(tuple(where))
    return drawn.at[spots[0]].set(smallest).at[spots[1]].set(largest)


def block_levels(stream_key, extent, cuts, smallest, high):
    loudness = 1.0
    for dim, parts in cuts:
        heights = jax.random.uniform(jax.random.fold_in(jax.random.fold_in(stream_key, 6), dim), (parts,), jnp.float32, smallest / len(cuts), high / len(cuts))
        loudness = loudness * jnp.repeat(jnp.exp(heights), extent[dim] // parts).reshape((-1,) + (1,) * (len(extent) - 1 - dim))
    return loudness


def bell_draw(own_key, shape, deviation, most, shards=(), held_as=jnp.bfloat16):
    drawn = deviation * jax.random.normal(own_key, shape, jnp.float32)
    if shards:
        drawn = drawn * block_levels(own_key, shape, shards, -0.22, 0.18)
    return jnp.clip(drawn, -most, most).astype(held_as)


def setup_inputs(seed: int = 0) -> dict:
    arg_keys = jax.random.split(jax.random.key(seed), 11)
    return {
        "density": bell_draw(arg_keys[0], (PANELS,), 1.0, 6.0, ((0, 512),), jnp.float32),
        "counts": draw_counts(jax.random.fold_in(arg_keys[10], 71), 0),
        "send_panel": place_ends(jax.random.randint(arg_keys[2], (DEVICES, DEVICES, CAP), 0, P_DEV), jax.random.fold_in(arg_keys[2], 1), 0, P_DEV - 1).astype(jnp.int32),
        "send_weight": bell_draw(arg_keys[3], (DEVICES, DEVICES, CAP), 0.6, 4.0, ((0, 512),), jnp.float32),
        "interp_weight": bell_draw(arg_keys[4], (DEVICES, DEVICES, CAP), 0.6, 4.0, ((0, 512),), jnp.float32),
        "recv_row": place_ends(jax.random.randint(arg_keys[5], (DEVICES, DEVICES, CAP), 0, CELLS_DEV), jax.random.fold_in(arg_keys[5], 1), 0, CELLS_DEV - 1).astype(jnp.int32),
        "recv_col": place_ends(jax.random.randint(arg_keys[6], (DEVICES, DEVICES, CAP), 0, NX), jax.random.fold_in(arg_keys[6], 1), 0, NX - 1).astype(jnp.int32),
        "kernel": draw_kernel(jax.random.fold_in(arg_keys[10], 71), 0),
        "near_index": place_ends(jax.random.randint(arg_keys[8], (NEAR, PANELS), 0, P_DEV * N_PATCH), jax.random.fold_in(arg_keys[8], 1), 0, (P_DEV * N_PATCH) - 1).astype(jnp.int32),
        "near_coef": bell_draw(arg_keys[9], (NEAR, PANELS), 0.15, 1.0, ((1, 512),), jnp.float32),
    }


def reference(density, counts, send_panel, send_weight, interp_weight, recv_row, recv_col, kernel, near_index, near_coef):
    devices = N_SLAB * N_PATCH
    slab_depth = NZ // N_SLAB
    patch_rows = NY // N_PATCH
    slots = jnp.arange(CAP, dtype=jnp.int32)
    in_use = slots[None, None, :] < counts[:, :, None]
    owners = jnp.arange(devices, dtype=jnp.int32)
    panels = owners[:, None, None] * P_DEV + send_panel
    items = jnp.where(in_use, send_weight * density[panels], 0.0)
    rows_in = jnp.transpose(recv_row, (1, 0, 2))
    columns_in = jnp.transpose(recv_col, (1, 0, 2))
    target = owners[None, :, None]
    depth = (target // N_PATCH) * slab_depth + rows_in // patch_rows
    across = (target % N_PATCH) * patch_rows + rows_in % patch_rows
    flat_cell = (depth * NY + across) * NX + columns_in
    grid = jnp.zeros((NZ * NY * NX,), jnp.float32).at[flat_cell.reshape(-1)].add(items.reshape(-1))
    spectrum = jnp.fft.fftn(grid.reshape(NZ, NY, NX)) * jnp.transpose(kernel, (2, 1, 0))
    field = jnp.real(jnp.fft.ifftn(spectrum)).astype(jnp.float32)
    sampled = field.reshape(-1)[flat_cell]
    terms = jnp.where(in_use, interp_weight * sampled, 0.0)
    interp = jnp.zeros((devices * P_DEV,), jnp.float32).at[panels.reshape(-1)].add(terms.reshape(-1))
    column = jnp.arange(devices * P_DEV, dtype=jnp.int32)
    group_base = (column // (N_PATCH * P_DEV)) * (N_PATCH * P_DEV)
    near = jnp.sum(near_coef * density[group_base[None, :] + near_index], axis=0)
    return interp + near
```

```python
import math

import jax
import jax.numpy as jnp
import ml_dtypes
import numpy as np
from jax import lax
from jax.experimental import pallas as pl
from jax.experimental.pallas import tpu as pltpu
from jax.sharding import PartitionSpec as P

NX, NY, NZ = 512, 512, 256
N_SLAB, N_PATCH, CAP = 64, 8, 8
DEVICES = N_SLAB * N_PATCH
F32, BF16, I32 = jnp.float32, jnp.bfloat16, jnp.int32
MIB = 1024 * 1024


def halves(table):
    high = table.astype(np.float32).astype(ml_dtypes.bfloat16)
    low = (table - high.astype(np.float64)).astype(np.float32).astype(ml_dtypes.bfloat16)
    return np.stack([high, low])


def waves(first, second, length):
    turns = np.outer(first, second) % length
    angles = turns * (2.0 * np.pi / length)
    cosine, sine = np.cos(angles), np.sin(angles)
    cosine[(4 * turns == length) | (4 * turns == 3 * length)] = 0.0
    sine[(turns == 0) | (2 * turns == length)] = 0.0
    return cosine, sine


def x_tables():
    cosine, sine = waves(np.arange(64), np.arange(64), 64)
    forward = np.block([[cosine, sine], [-sine, cosine]])
    backward = np.block([[cosine, -sine], [sine, cosine]])
    return halves(forward), halves(backward)


def y_tables():
    cosine, sine = waves(np.arange(NY), np.arange(NY // 2), NY)
    sine[:, 0] = 1.0 - 2.0 * (np.arange(NY) % 2)
    return halves(np.concatenate([cosine, sine], axis=1)), halves(np.concatenate([cosine.T, sine.T], axis=0))


def z_tables():
    cosine, sine = waves(np.arange(NZ), np.arange(NZ), NZ)
    depth = NZ // N_SLAB

    def rows(re_part, im_part):
        parts = np.stack([re_part.reshape(N_SLAB, depth, -1), im_part.reshape(N_SLAB, depth, -1)], axis=1)
        return parts.reshape(2 * NZ, -1)

    forward = np.concatenate([rows(cosine, sine), rows(-sine, cosine)], axis=1).T
    backward = np.concatenate([rows(cosine, sine), rows(-sine, cosine)], axis=1)
    return halves(forward), halves(backward)


def split(value):
    high = value.astype(BF16)
    return high, (value - high.astype(F32)).astype(BF16)


def mul(a, b):
    return jnp.dot(a, b, preferred_element_type=F32)


def data_by_table(value, table_ref):
    high, low = split(value)
    return mul(high, table_ref[0]) + mul(low, table_ref[0]) + mul(high, table_ref[1])


def table_by_data(table_ref, value):
    high, low = split(value)
    return mul(table_ref[0], high) + mul(table_ref[0], low) + mul(table_ref[1], high)


def across(a, b):
    return lax.dot_general(
        a, b, (((1,), (1,)), ((), ())), precision=lax.Precision.HIGHEST, preferred_element_type=F32
    )


def iota(shape, dim):
    return lax.broadcasted_iota(I32, shape, dim)


def spread(values):
    keep = (iota((8, DEVICES), 1) & 7) == iota((8, DEVICES), 0)
    rows = [jnp.where(keep, jnp.broadcast_to(values[c : c + 1, :], (8, DEVICES)), 0.0) for c in range(CAP)]
    return jnp.concatenate(rows, axis=0)


def slab_of():
    return ((iota((N_SLAB, DEVICES), 1) >> 3) == iota((N_SLAB, DEVICES), 0)).astype(F32)


def paired(values):
    rows = [
        jnp.concatenate([values[16 * q : 16 * q + 8, :], values[16 * q + 8 : 16 * q + 16, :]], axis=1)
        for q in range(CAP // 2)
    ]
    return jnp.concatenate(rows, axis=0)


def unpaired(values):
    rows = []
    for q in range(CAP // 2):
        rows.append(values[8 * q : 8 * q + 8, :64])
        rows.append(values[8 * q : 8 * q + 8, 64:])
    return jnp.concatenate(rows, axis=0)


def lookup(row, places):
    return jnp.take_along_axis(
        jnp.broadcast_to(row, places.shape), places, axis=1, mode="promise_in_bounds"
    )


def items_kernel(density, counts, panel, weight, row, col, out, cells):
    used = iota((CAP, DEVICES), 0) < counts[...]
    picked = []
    for j in range(4):
        places = panel[:, 128 * j : 128 * (j + 1)]
        low, high = places & 127, places >> 7
        value = jnp.zeros(places.shape, F32)
        for h in range(4):
            value = jnp.where(high == h, lookup(density[h : h + 1, :], low), value)
        picked.append(value)
    items = jnp.where(used, weight[...] * jnp.concatenate(picked, axis=1), 0.0)
    slab = slab_of()
    out[:, 0, :] = across(slab, spread(items))
    place = (row[...] * NX + col[...]).astype(F32)
    cells[...] = paired(across(spread(place), slab))


def message_kernel(arrived, cells, density, out):
    items = paired(arrived[:, 0, :].T)
    for p in range(N_PATCH):
        out[p, 0:32, :] = items
        out[p, 32:64, :] = cells[...]
        out[p, 64:68, :] = density[...]
        out[p, 68:72, :] = density[...]


def phases(cell, p):
    place = (cell + 0.5).astype(I32)
    col = place & (NX - 1)
    angle = ((col * p) & (NX - 1)).astype(F32) * (2.0 * math.pi / NX)
    return (place >> 9).astype(F32), (col & 63).astype(F32), jnp.cos(angle), jnp.sin(angle)


def lanes(ref, block, p, kind=0):
    rows = [ref[kind, block, pl.ds(8 * q + p, 1), :] for q in range(4)]
    return jnp.concatenate(rows, axis=1)


def thick(row, count):
    return jnp.concatenate([jnp.broadcast_to(row, (16, row.shape[1])).astype(BF16)] * count, axis=0)


def one_hot(row, count, size):
    steps = lax.broadcasted_iota(I32, (size, row.shape[1]), 0).astype(F32).astype(BF16)
    return thick(row, count) == steps


def forward_kernel(meta, data, x_table, y_table, out, slots, lines):
    p = meta[0]
    for q in range(4):
        for sender in range(N_PATCH):
            slots[4, :, 8 * q + sender, :] = data[sender, 8 * q : 8 * q + 8, :]
    for block in range(N_PATCH):
        row, low_col, cosine, sine = phases(data[block, 32:64, :], p)
        slots[0, block] = row
        slots[1, block] = low_col
        slots[2, block] = slots[4, block] * cosine
        slots[3, block] = -slots[4, block] * sine

    def one_block(block, carry):
        total = jnp.zeros((256, 256), F32)
        for sender in range(N_PATCH):
            in_row = one_hot(lanes(slots, block, sender, 0), 16, 256)
            in_col = one_hot(lanes(slots, block, sender, 1), 4, 64)
            none = jnp.zeros((64, 512), BF16)
            re_high, re_low = split(lanes(slots, block, sender, 2))
            im_high, im_low = split(lanes(slots, block, sender, 3))
            parts = [jnp.where(in_col, thick(v.astype(F32), 4), none) for v in (re_high, im_high, re_low, im_low)]
            ones = jnp.where(in_row, jnp.ones((256, 512), BF16), jnp.zeros((256, 512), BF16))
            total = total + lax.dot_general(
                jnp.concatenate(parts, axis=0),
                ones,
                (((1,), (1,)), ((), ())),
                preferred_element_type=F32,
            )
        lines[block] = table_by_data(x_table, total[:128, :] + total[128:, :])
        return carry

    lax.fori_loop(0, N_PATCH, one_block, 0)
    lower = iota((128, 128), 1) < 64
    kx = 8 * iota((64, 256), 0) + p
    first = iota((64, 256), 1) == 0
    alone = (kx == 0) | (kx == NX // 2)
    for z in range(4):
        at = slice(128 * (z // 2), 128 * (z // 2) + 128)
        tiles = []
        for t in range(4):
            even, odd = lines[2 * t, :, at], lines[2 * t + 1, :, at]
            if z % 2 == 0:
                tiles.append(jnp.where(lower, even, pltpu.roll(odd, 64, 1)))
            else:
                tiles.append(jnp.where(lower, pltpu.roll(even, 64, 1), odd))
        both = data_by_table(jnp.concatenate(tiles, axis=1), y_table)
        re_cos, re_sin = both[:64, :256], both[:64, 256:]
        im_cos, im_sin = both[64:, :256], both[64:, 256:]
        re_first = jnp.where(kx <= NX // 2, re_cos, re_sin)
        im_first = jnp.where(alone, re_sin, jnp.where(kx < NX // 2, im_cos, im_sin))
        out[:, z, :] = jnp.where(first, re_first, re_cos + im_sin)
        out[:, 4 + z, :] = jnp.where(first, im_first, im_cos - re_sin)


def spectrum_kernel(factor, kernel, lines, forward, backward, out):
    size = NY // 2
    green = kernel[0, :size, :].T
    base = factor[4]
    low, mid = kernel[0, 0:8, :].T[:, 0:1], kernel[0, size : size + 8, :].T[:, 0:1]
    first = iota((NZ, size), 1) == 0
    own = jnp.where(first, factor[0] * low + factor[1] * mid, base * green)
    mirrored = jnp.where(first[:, :128], factor[2] * low + factor[3] * mid, 0.0)
    value = lines[...].reshape(2 * NZ, size)
    sign = jnp.where((iota((2 * NZ, 128), 0) & 4) == 0, 1.0, -1.0)
    wave = table_by_data(forward, value)
    turned = table_by_data(forward, value[:, :128] * sign)
    left = jnp.concatenate([own[:, :128]] * 2, axis=0) * wave[:, :128]
    left = left + jnp.concatenate([mirrored] * 2, axis=0) * turned
    right = jnp.concatenate([own[:, 128:]] * 2, axis=0) * wave[:, 128:]
    scaled = jnp.concatenate([left, right], axis=1)
    out[...] = table_by_data(backward, scaled).reshape(N_SLAB, 8, size)


def backward_kernel(meta, arrived, data, x_table, y_table, out, slots, planes, blocks):
    p = meta[0]
    for block in range(N_PATCH):
        row, low_col, cosine, sine = phases(data[block, 32:64, :], p)
        slots[0, block] = row
        slots[1, block] = low_col
        slots[2, block] = cosine
        slots[3, block] = sine
    value = arrived[...].reshape(512, 256)
    place = iota((512, 256), 0)
    real = (place & 4) == 0
    kx = 8 * (place >> 3) + p
    first = iota((512, 256), 1) == 0
    alone = (kx == 0) | (kx == NX // 2)
    after, before = pltpu.roll(value, 508, 0), pltpu.roll(value, 4, 0)
    keep = (kx <= NX // 2) & (real | ~alone)
    straight = jnp.where(first & ~keep, 0.0, value)
    other = jnp.where(kx > NX // 2, value, jnp.where(alone & real, after, 0.0))
    crossed = jnp.where(first, other, jnp.where(real, -after, before))
    planes[...] = data_by_table(jnp.concatenate([straight, crossed], axis=1), y_table).reshape(64, 8, 512)
    lower = iota((128, 128), 1) < 64
    for pair in range(2):
        plane = []
        for z in (2 * pair, 2 * pair + 1):
            both = jnp.concatenate([planes[:, z, :], planes[:, 4 + z, :]], axis=0)
            plane.append(table_by_data(x_table, both))
        for t in range(4):
            even = plane[0][:, 128 * t : 128 * (t + 1)]
            odd = plane[1][:, 128 * t : 128 * (t + 1)]
            for block, tile in (
                (2 * t, jnp.where(lower, even, pltpu.roll(odd, 64, 1))),
                (2 * t + 1, jnp.where(lower, pltpu.roll(even, 64, 1), odd)),
            ):
                high, low = split(tile)
                blocks[block, :128, 128 * pair : 128 * (pair + 1)] = high
                blocks[block, 128:, 128 * pair : 128 * (pair + 1)] = low

    steps = iota((64, 512), 0).astype(F32)

    def one_block(block, carry):
        field = blocks[block]
        for sender in range(N_PATCH):
            in_row = one_hot(lanes(slots, block, sender, 0), 16, 256)
            ones = jnp.where(in_row, jnp.ones((256, 512), BF16), jnp.zeros((256, 512), BF16))
            near = mul(field, ones)
            re_part = near[0:64] + near[128:192]
            im_part = near[64:128] + near[192:256]
            turned = re_part * lanes(slots, block, sender, 2) - im_part * lanes(slots, block, sender, 3)
            in_col = lanes(slots, block, sender, 1) == steps
            found = jnp.sum(jnp.where(in_col, turned, 0.0), axis=0, keepdims=True)
            for q in range(4):
                out[sender, pl.ds(8 * q + block, 1), :] = found[:, 128 * q : 128 * (q + 1)]
        return carry

    lax.fori_loop(0, N_PATCH, one_block, 0)


def sum_kernel(parts, out):
    total = parts[0]
    for p in range(1, N_PATCH):
        total = total + parts[p]
    out[:, 0, :] = unpaired(total).T


def near_kernel(data, index, coef, out):
    for j in range(4):
        at = slice(128 * j, 128 * (j + 1))
        total = jnp.zeros((8, 128), F32)
        for half in range(2):
            places = index[8 * half : 8 * half + 8, at]
            low, high = places & 127, places >> 7
            value = jnp.zeros(places.shape, F32)
            for h in range(32):
                value = jnp.where(high == h, lookup(data[h // 4, 64 + h % 4 : 65 + h % 4, :], low), value)
            total = total + coef[8 * half : 8 * half + 8, at] * value
        out[j : j + 1, :] = jnp.sum(total, axis=0, keepdims=True)


def interp_kernel(arrived, counts, panel, weight, near, out):
    used = iota((CAP, DEVICES), 0) < counts[...]
    wide = across(arrived[:, 0, :].T, slab_of().T)
    keep = (iota((64, DEVICES), 1) & 7) == (iota((64, DEVICES), 0) & 7)
    wide = jnp.where(keep, wide, 0.0)
    rows = [jnp.sum(wide[8 * c : 8 * c + 8, :], axis=0, keepdims=True) for c in range(CAP)]
    terms = jnp.where(used, weight[...] * jnp.concatenate(rows, axis=0), 0.0)
    places = panel[...]
    low, high = places & 127, places >> 7
    total = jnp.zeros((16, 128), F32)
    part = iota((16, DEVICES), 0)
    for c in range(CAP):
        term = terms[c : c + 1, :]
        top = term.astype(BF16).astype(F32)
        middle = (term - top).astype(BF16).astype(F32)
        bottom = term - top - middle
        shown = jnp.where(part < 4, top, jnp.where(part < 8, middle, jnp.where(part < 12, bottom, 0.0)))
        left = jnp.where((part & 3) == high[c : c + 1, :], shown, 0.0).astype(BF16)
        right = (iota((128, DEVICES), 0) == low[c : c + 1, :]).astype(F32).astype(BF16)
        total = total + lax.dot_general(left, right, (((1,), (1,)), ((), ())), preferred_element_type=F32)
    out[...] = total[0:4] + total[4:8] + total[8:12] + near[...]


VMEM = pl.BlockSpec(memory_space=pltpu.VMEM)
SMEM = pl.BlockSpec(memory_space=pltpu.SMEM)


def call(kernel, shapes, args, scratch=(), scalars=0, vmem=16, flops=0):
    many = isinstance(shapes, list)
    outs = [jax.ShapeDtypeStruct(s, F32) for s in (shapes if many else [shapes])]
    moved = 4 * sum(math.prod(o.shape) for o in outs) + sum(a.size * a.dtype.itemsize for a in args)
    return pl.pallas_call(
        kernel,
        out_shape=outs if many else outs[0],
        in_specs=[SMEM] * scalars + [VMEM] * (len(args) - scalars),
        out_specs=[VMEM] * len(outs) if many else VMEM,
        scratch_shapes=list(scratch),
        compiler_params=pltpu.CompilerParams(vmem_limit_bytes=vmem * MIB),
        cost_estimate=pl.CostEstimate(flops=flops, bytes_accessed=moved, transcendentals=0),
    )(*args)


def exchange(value, axis):
    return lax.all_to_all(value, axis, split_axis=0, concat_axis=0, tiled=True)


def per_device(
    density,
    counts,
    send_panel,
    send_weight,
    interp_weight,
    recv_row,
    recv_col,
    kernel,
    near_index,
    near_coef,
):
    p = lax.axis_index("patch").astype(I32)
    own = lax.axis_index("slab").astype(I32) * N_PATCH + p
    meta = jnp.stack([p, own])
    x_forward, x_backward = (jnp.asarray(t) for t in x_tables())
    y_forward, y_backward = (jnp.asarray(t) for t in y_tables())
    z_forward, z_backward = (jnp.asarray(t) for t in z_tables())
    charge = density.reshape(4, 128)
    panel, weight, back_weight, row, col = (
        jnp.transpose(a[0]) for a in (send_panel, send_weight, interp_weight, recv_row, recv_col)
    )

    items, cells = call(
        items_kernel, [(N_SLAB, 1, 64), (32, 128)], [charge, counts, panel, weight, row, col]
    )
    arrived = exchange(items, "slab")
    message = call(message_kernel, (N_PATCH, 72, 128), [arrived, cells, charge])
    data = exchange(message, "patch")
    near = call(near_kernel, (4, 128), [data, near_index, near_coef])

    lines = call(
        forward_kernel,
        (N_SLAB, 8, 256),
        [meta, data, x_forward, y_forward],
        [pltpu.VMEM((5, N_PATCH, 32, 128), F32), pltpu.VMEM((N_PATCH, 128, 256), F32)],
        scalars=1,
        vmem=32,
    )
    lines = exchange(lines, "slab")

    unit = 2.0 / (NX * NY * NZ)
    alone = (own == 0) | (own == NX // 2)
    below = own < NX // 2
    factor = jnp.stack(
        [
            jnp.where(alone, 0.25 * unit, jnp.where(below, unit, 0.0)),
            jnp.where(alone, 0.25 * unit, jnp.where(below, 0.0, unit)),
            jnp.where(alone, 0.25 * unit, 0.0),
            jnp.where(alone, -0.25 * unit, 0.0),
            jnp.full((), unit, F32),
        ]
    ).astype(F32)
    lines = call(
        spectrum_kernel,
        (N_SLAB, 8, 256),
        [factor, kernel, lines, z_forward, z_backward],
        scalars=1,
        vmem=24,
    )
    lines = exchange(lines, "slab")
    parts = call(
        backward_kernel,
        (N_PATCH, 32, 128),
        [meta, lines, data, x_backward, y_backward],
        [
            pltpu.VMEM((4, N_PATCH, 32, 128), F32),
            pltpu.VMEM((N_SLAB, 8, 512), F32),
            pltpu.VMEM((N_PATCH, 256, 256), BF16),
        ],
        scalars=1,
        vmem=32,
    )
    parts = exchange(parts, "patch")
    sampled = call(sum_kernel, (N_SLAB, 1, 64), [parts])
    sampled = exchange(sampled, "slab")
    result = call(interp_kernel, (4, 128), [sampled, counts, panel, back_weight, near])
    return result.reshape(-1)


def solution(mesh):
    placed = (
        P(("slab", "patch")),
        P(("slab", "patch"), None),
        P(("slab", "patch"), None, None),
        P(("slab", "patch"), None, None),
        P(("slab", "patch"), None, None),
        P(("slab", "patch"), None, None),
        P(("slab", "patch"), None, None),
        P(("slab", "patch"), None, None),
        P(None, ("slab", "patch")),
        P(None, ("slab", "patch")),
    )
    return jax.shard_map(
        per_device, mesh=mesh, in_specs=placed, out_specs=P(("slab", "patch")), check_vma=False
    )
```

```python
import math

import jax
import jax.numpy as jnp
import ml_dtypes
import numpy as np
from jax import lax
from jax.experimental import pallas as pl
from jax.experimental.pallas import tpu as pltpu
from jax.sharding import PartitionSpec as P

NX, NY, NZ = 512, 512, 256
N_SLAB, N_PATCH, CAP = 64, 8, 8
DEVICES = N_SLAB * N_PATCH
F32, BF16, I32 = jnp.float32, jnp.bfloat16, jnp.int32
MIB = 1024 * 1024


def halves(table):
    high = table.astype(np.float32).astype(ml_dtypes.bfloat16)
    low = (table - high.astype(np.float64)).astype(np.float32).astype(ml_dtypes.bfloat16)
    return np.stack([high, low])


def wide(table):
    high, low = halves(table)
    return np.concatenate([high, high, low], axis=1)


def waves(first, second, length):
    turns = np.outer(first, second) % length
    angles = turns * (2.0 * np.pi / length)
    cosine, sine = np.cos(angles), np.sin(angles)
    cosine[(4 * turns == length) | (4 * turns == 3 * length)] = 0.0
    sine[(turns == 0) | (2 * turns == length)] = 0.0
    return cosine, sine


def x_tables():
    cosine, sine = waves(np.arange(64), np.arange(64), 64)
    forward = np.block([[cosine, sine], [-sine, cosine]])
    backward = np.block([[cosine, -sine], [sine, cosine]])
    return wide(forward), wide(backward)


def y_tables():
    cosine, sine = waves(np.arange(NY), np.arange(NY // 2), NY)
    sine[:, 0] = 1.0 - 2.0 * (np.arange(NY) % 2)
    return halves(np.concatenate([cosine, sine], axis=1)), halves(np.concatenate([cosine.T, sine.T], axis=0))


def z_tables():
    cosine, sine = waves(np.arange(NZ), np.arange(NZ), NZ)
    depth = NZ // N_SLAB

    def rows(re_part, im_part):
        parts = np.stack([re_part.reshape(N_SLAB, depth, -1), im_part.reshape(N_SLAB, depth, -1)], axis=1)
        return parts.reshape(2 * NZ, -1)

    forward = np.concatenate([rows(cosine, sine), rows(-sine, cosine)], axis=1).T
    backward = np.concatenate([rows(cosine, sine), rows(-sine, cosine)], axis=1)
    return halves(forward), halves(backward)


def quarter_table():
    cosine, sine = waves(np.arange(128), np.ones(1, np.int64), NX)
    return np.stack([cosine[:, 0], sine[:, 0]]).astype(np.float32)


def split(value):
    high = value.astype(BF16)
    return high, (value - high.astype(F32)).astype(BF16)


def mul(a, b):
    return jnp.dot(a, b, preferred_element_type=F32)


def data_by_table(value, table_ref):
    high, low = split(value)
    return mul(high, table_ref[0]) + mul(low, table_ref[0]) + mul(high, table_ref[1])


def table_by_data(table_ref, value):
    high, low = split(value)
    return mul(table_ref[0], high) + mul(table_ref[0], low) + mul(table_ref[1], high)


def wide_by_data(table_ref, value):
    high, low = split(value)
    return mul(table_ref[...], jnp.concatenate([high, low, high], axis=0))


def across(a, b):
    return lax.dot_general(
        a, b, (((1,), (1,)), ((), ())), precision=lax.Precision.HIGHEST, preferred_element_type=F32
    )


def iota(shape, dim):
    return lax.broadcasted_iota(I32, shape, dim)


def spread(values):
    keep = (iota((8, DEVICES), 1) & 7) == iota((8, DEVICES), 0)
    rows = [jnp.where(keep, jnp.broadcast_to(values[c : c + 1, :], (8, DEVICES)), 0.0) for c in range(CAP)]
    return jnp.concatenate(rows, axis=0)


def slab_of():
    return ((iota((N_SLAB, DEVICES), 1) >> 3) == iota((N_SLAB, DEVICES), 0)).astype(F32)


def paired(values):
    rows = [
        jnp.concatenate([values[16 * q : 16 * q + 8, :], values[16 * q + 8 : 16 * q + 16, :]], axis=1)
        for q in range(CAP // 2)
    ]
    return jnp.concatenate(rows, axis=0)


def unpaired(values):
    rows = []
    for q in range(CAP // 2):
        rows.append(values[8 * q : 8 * q + 8, :64])
        rows.append(values[8 * q : 8 * q + 8, 64:])
    return jnp.concatenate(rows, axis=0)


def lookup(row, places):
    return jnp.take_along_axis(
        jnp.broadcast_to(row, places.shape), places, axis=1, mode="promise_in_bounds"
    )


def items_kernel(*refs):
    sources, (out, message), held, (told, done, sent) = refs[:6], refs[6:8], refs[8:14], refs[14:]
    copies = [pltpu.make_async_copy(a, b, done.at[k]) for k, (a, b) in enumerate(zip(sources, held))]
    for copy in copies:
        copy.start()
    density, counts, panel, weight, row, col = held
    for copy in copies:
        copy.wait()
    slab = slab_of()
    place = (row[...] * NX + col[...]).astype(F32)
    told[0:32, :] = paired(across(spread(place), slab))
    told[32:36, :] = density[...]
    told[36:40, :] = density[...]
    copies = [pltpu.make_async_copy(told, message.at[p, 32:72], sent.at[p]) for p in range(N_PATCH)]
    for copy in copies:
        copy.start()
    used = iota((CAP, DEVICES), 0) < counts[...]
    picked = []
    for j in range(4):
        places = panel[:, 128 * j : 128 * (j + 1)]
        low, high = places & 127, places >> 7
        value = jnp.zeros(places.shape, F32)
        for h in range(4):
            value = jnp.where(high == h, lookup(density[h : h + 1, :], low), value)
        picked.append(value)
    items = jnp.where(used, weight[...] * jnp.concatenate(picked, axis=1), 0.0)
    out[:, 0, :] = across(slab, spread(items))
    for copy in copies:
        copy.wait()


def message_kernel(arrived, message, out, items, sent):
    del message
    items[...] = paired(arrived[:, 0, :].T)
    copies = [pltpu.make_async_copy(items, out.at[p, 0:32], sent.at[p]) for p in range(N_PATCH)]
    for copy in copies:
        copy.start()
    for copy in copies:
        copy.wait()


def phases(cell, p, quarter):
    place = (cell + 0.5).astype(I32)
    col = place & (NX - 1)
    turn = (col * p) & (NX - 1)
    part, within = turn >> 7, turn & 127
    cosine, sine = lookup(quarter[0:1, :], within), lookup(quarter[1:2, :], within)
    odd = (part & 1) == 1
    real, imag = jnp.where(odd, sine, cosine), jnp.where(odd, cosine, sine)
    real = jnp.where((part == 1) | (part == 2), -real, real)
    imag = jnp.where(part >= 2, -imag, imag)
    return (place >> 9).astype(F32), (col & 63).astype(F32), real, imag


def lanes(ref, block, p, kind=0):
    rows = [ref[kind, block, 8 * q + p : 8 * q + p + 1, :] for q in range(4)]
    return jnp.concatenate(rows, axis=1)


def thick(row, count):
    return jnp.concatenate([jnp.broadcast_to(row, (16, row.shape[1])).astype(BF16)] * count, axis=0)


def one_hot(row, count, size):
    steps = lax.broadcasted_iota(I32, (size, row.shape[1]), 0).astype(F32).astype(BF16)
    return thick(row, count) == steps


def forward_kernel(meta, data, quarter, x_table, y_table, out, slots, lines):
    p = meta[0]
    for q in range(4):
        for sender in range(N_PATCH):
            slots[4, :, 8 * q + sender, :] = data[sender, 8 * q : 8 * q + 8, :]
    for block in range(N_PATCH):
        row, low_col, cosine, sine = phases(data[block, 32:64, :], p, quarter)
        slots[0, block] = row
        slots[1, block] = low_col
        slots[2, block] = slots[4, block] * cosine
        slots[3, block] = -slots[4, block] * sine

    for block in range(N_PATCH):
        total = jnp.zeros((256, 256), F32)
        for sender in range(N_PATCH):
            in_row = one_hot(lanes(slots, block, sender, 0), 16, 256)
            in_col = one_hot(lanes(slots, block, sender, 1), 4, 64)
            none = jnp.zeros((64, 512), BF16)
            re_high, re_low = split(lanes(slots, block, sender, 2))
            im_high, im_low = split(lanes(slots, block, sender, 3))
            parts = [jnp.where(in_col, thick(v.astype(F32), 4), none) for v in (re_high, im_high, re_low, im_low)]
            ones = jnp.where(in_row, jnp.ones((256, 512), BF16), jnp.zeros((256, 512), BF16))
            total = total + lax.dot_general(
                jnp.concatenate(parts, axis=0),
                ones,
                (((1,), (1,)), ((), ())),
                preferred_element_type=F32,
            )
        lines[block] = total[:128, :] + total[128:, :]
    waved = wide_by_data(x_table, jnp.concatenate([lines[b] for b in range(N_PATCH)], axis=1))
    lower = iota((128, 128), 1) < 64
    rows = []
    for z in range(4):
        tiles = []
        for t in range(4):
            start = 512 * t + 128 * (z // 2)
            even, odd = waved[:, start : start + 128], waved[:, start + 256 : start + 384]
            if z % 2 == 0:
                tiles.append(jnp.where(lower, even, pltpu.roll(odd, 64, 1)))
            else:
                tiles.append(jnp.where(lower, pltpu.roll(even, 64, 1), odd))
        rows.append(jnp.concatenate(tiles, axis=1))
    both = data_by_table(jnp.concatenate(rows, axis=0), y_table)
    kx = 8 * iota((64, 256), 0) + p
    first = iota((64, 256), 1) == 0
    alone = (kx == 0) | (kx == NX // 2)
    for z in range(4):
        real, imag = both[128 * z : 128 * z + 64], both[128 * z + 64 : 128 * z + 128]
        re_cos, re_sin = real[:, :256], real[:, 256:]
        im_cos, im_sin = imag[:, :256], imag[:, 256:]
        re_first = jnp.where(kx <= NX // 2, re_cos, re_sin)
        im_first = jnp.where(alone, re_sin, jnp.where(kx < NX // 2, im_cos, im_sin))
        out[:, z, :] = jnp.where(first, re_first, re_cos + im_sin)
        out[:, 4 + z, :] = jnp.where(first, im_first, im_cos - re_sin)


def spectrum_kernel(factor, kernel, lines, forward, backward, out):
    size = NY // 2
    green = kernel[0, :size, :].T
    base = factor[4]
    low, mid = kernel[0, 0:8, :].T[:, 0:1], kernel[0, size : size + 8, :].T[:, 0:1]
    first = iota((NZ, size), 1) == 0
    own = jnp.where(first, factor[0] * low + factor[1] * mid, base * green)
    mirrored = jnp.where(first[:, :128], factor[2] * low + factor[3] * mid, 0.0)
    value = lines[...].reshape(2 * NZ, size)
    sign = jnp.where((iota((2 * NZ, 128), 0) & 4) == 0, 1.0, -1.0)
    wave = table_by_data(forward, value)
    turned = table_by_data(forward, value[:, :128] * sign)
    left = jnp.concatenate([own[:, :128]] * 2, axis=0) * wave[:, :128]
    left = left + jnp.concatenate([mirrored] * 2, axis=0) * turned
    right = jnp.concatenate([own[:, 128:]] * 2, axis=0) * wave[:, 128:]
    scaled = jnp.concatenate([left, right], axis=1)
    out[...] = table_by_data(backward, scaled).reshape(N_SLAB, 8, size)


def backward_kernel(meta, arrived, data, quarter, x_table, y_table, out, slots, planes, blocks):
    p = meta[0]
    for block in range(N_PATCH):
        row, low_col, cosine, sine = phases(data[block, 32:64, :], p, quarter)
        slots[0, block] = row
        slots[1, block] = low_col
        slots[2, block] = cosine
        slots[3, block] = sine
    value = arrived[...].reshape(512, 256)
    place = iota((512, 256), 0)
    real = (place & 4) == 0
    kx = 8 * (place >> 3) + p
    first = iota((512, 256), 1) == 0
    alone = (kx == 0) | (kx == NX // 2)
    after, before = pltpu.roll(value, 508, 0), pltpu.roll(value, 4, 0)
    keep = (kx <= NX // 2) & (real | ~alone)
    straight = jnp.where(first & ~keep, 0.0, value)
    other = jnp.where(kx > NX // 2, value, jnp.where(alone & real, after, 0.0))
    crossed = jnp.where(first, other, jnp.where(real, -after, before))
    planes[...] = data_by_table(jnp.concatenate([straight, crossed], axis=1), y_table).reshape(64, 8, 512)
    lower = iota((128, 128), 1) < 64
    both = [jnp.concatenate([planes[:, z, :], planes[:, 4 + z, :]], axis=0) for z in range(4)]
    waved = wide_by_data(x_table, jnp.concatenate(both, axis=1))
    for pair in range(2):
        for t in range(4):
            start = 1024 * pair + 128 * t
            even, odd = waved[:, start : start + 128], waved[:, start + 512 : start + 640]
            for block, tile in (
                (2 * t, jnp.where(lower, even, pltpu.roll(odd, 64, 1))),
                (2 * t + 1, jnp.where(lower, pltpu.roll(even, 64, 1), odd)),
            ):
                high, low = split(tile)
                blocks[block, :128, 128 * pair : 128 * (pair + 1)] = high
                blocks[block, 128:, 128 * pair : 128 * (pair + 1)] = low

    steps = iota((64, 512), 0).astype(F32)

    for block in range(N_PATCH):
        field = blocks[block]
        for sender in range(N_PATCH):
            in_row = one_hot(lanes(slots, block, sender, 0), 16, 256)
            ones = jnp.where(in_row, jnp.ones((256, 512), BF16), jnp.zeros((256, 512), BF16))
            near = mul(field, ones)
            re_part = near[0:64] + near[128:192]
            im_part = near[64:128] + near[192:256]
            turned = re_part * lanes(slots, block, sender, 2) - im_part * lanes(slots, block, sender, 3)
            in_col = lanes(slots, block, sender, 1) == steps
            found = jnp.sum(jnp.where(in_col, turned, 0.0), axis=0, keepdims=True)
            for q in range(4):
                out[sender, 8 * q + block : 8 * q + block + 1, :] = found[:, 128 * q : 128 * (q + 1)]


def sum_kernel(parts, out):
    total = parts[0]
    for p in range(1, N_PATCH):
        total = total + parts[p]
    out[:, 0, :] = unpaired(total).T


def near_kernel(data, index, coef, out):
    for j in range(4):
        at = slice(128 * j, 128 * (j + 1))
        total = jnp.zeros((8, 128), F32)
        for half in range(2):
            places = index[8 * half : 8 * half + 8, at]
            low, high = places & 127, places >> 7
            value = jnp.zeros(places.shape, F32)
            for h in range(32):
                value = jnp.where(high == h, lookup(data[h // 4, 64 + h % 4 : 65 + h % 4, :], low), value)
            total = total + coef[8 * half : 8 * half + 8, at] * value
        out[j : j + 1, :] = jnp.sum(total, axis=0, keepdims=True)


def interp_kernel(arrived, counts, panel, weight, near, out):
    used = iota((CAP, DEVICES), 0) < counts[...]
    wide = across(arrived[:, 0, :].T, slab_of().T)
    keep = (iota((64, DEVICES), 1) & 7) == (iota((64, DEVICES), 0) & 7)
    wide = jnp.where(keep, wide, 0.0)
    rows = [jnp.sum(wide[8 * c : 8 * c + 8, :], axis=0, keepdims=True) for c in range(CAP)]
    terms = jnp.where(used, weight[...] * jnp.concatenate(rows, axis=0), 0.0)
    places = panel[...]
    low, high = places & 127, places >> 7
    total = jnp.zeros((16, 128), F32)
    part = iota((16, DEVICES), 0)
    for c in range(CAP):
        term = terms[c : c + 1, :]
        top = term.astype(BF16).astype(F32)
        middle = (term - top).astype(BF16).astype(F32)
        bottom = term - top - middle
        shown = jnp.where(part < 4, top, jnp.where(part < 8, middle, jnp.where(part < 12, bottom, 0.0)))
        left = jnp.where((part & 3) == high[c : c + 1, :], shown, 0.0).astype(BF16)
        right = (iota((128, DEVICES), 0) == low[c : c + 1, :]).astype(F32).astype(BF16)
        total = total + lax.dot_general(left, right, (((1,), (1,)), ((), ())), preferred_element_type=F32)
    out[...] = total[0:4] + total[4:8] + total[8:12] + near[...]


VMEM = pl.BlockSpec(memory_space=pltpu.VMEM)
SMEM = pl.BlockSpec(memory_space=pltpu.SMEM)
FAR = pl.BlockSpec(memory_space=pltpu.HBM)


def call(kernel, shapes, args, scratch=(), scalars=0, vmem=16, sources=None, outs=VMEM, aliases=None):
    many = isinstance(shapes, list)
    shape = [jax.ShapeDtypeStruct(s, F32) for s in (shapes if many else [shapes])]
    moved = 4 * sum(math.prod(o.shape) for o in shape) + sum(a.size * a.dtype.itemsize for a in args)
    return pl.pallas_call(
        kernel,
        out_shape=shape if many else shape[0],
        in_specs=sources or [SMEM] * scalars + [VMEM] * (len(args) - scalars),
        out_specs=outs,
        scratch_shapes=list(scratch),
        input_output_aliases=aliases or {},
        compiler_params=pltpu.CompilerParams(vmem_limit_bytes=vmem * MIB),
        cost_estimate=pl.CostEstimate(flops=0, bytes_accessed=moved, transcendentals=0),
    )(*args)


def run_items(*args):
    held = [pltpu.VMEM(a.shape, a.dtype) for a in args]
    return call(
        items_kernel,
        [(N_SLAB, 1, 64), (N_PATCH, 72, 128)],
        args,
        held + [pltpu.VMEM((40, 128), F32), pltpu.SemaphoreType.DMA((6,)), pltpu.SemaphoreType.DMA((8,))],
        vmem=60,
        sources=[FAR] * 6,
        outs=[VMEM, FAR],
    )


def run_message(arrived, message):
    return call(
        message_kernel,
        (N_PATCH, 72, 128),
        [arrived, message],
        [pltpu.VMEM((32, 128), F32), pltpu.SemaphoreType.DMA((8,))],
        vmem=60,
        sources=[VMEM, FAR],
        outs=FAR,
        aliases={1: 0},
    )


def exchange(value, axis):
    return lax.all_to_all(value, axis, split_axis=0, concat_axis=0, tiled=True)


def run_forward(meta, data, quarter, x_table, y_table):
    return call(
        forward_kernel,
        (N_SLAB, 8, 256),
        [meta, data, quarter, x_table, y_table],
        [pltpu.VMEM((5, N_PATCH, 32, 128), F32), pltpu.VMEM((N_PATCH, 128, 256), F32)],
        scalars=1,
        vmem=32,
    )


def run_spectrum(factor, kernel, lines, forward, backward):
    return call(
        spectrum_kernel, (N_SLAB, 8, 256), [factor, kernel, lines, forward, backward], scalars=1, vmem=24
    )


def run_backward(meta, lines, data, quarter, x_table, y_table):
    return call(
        backward_kernel,
        (N_PATCH, 32, 128),
        [meta, lines, data, quarter, x_table, y_table],
        [
            pltpu.VMEM((4, N_PATCH, 32, 128), F32),
            pltpu.VMEM((N_SLAB, 8, 512), F32),
            pltpu.VMEM((N_PATCH, 256, 256), BF16),
        ],
        scalars=1,
        vmem=32,
    )


def per_device(
    density,
    counts,
    send_panel,
    send_weight,
    interp_weight,
    recv_row,
    recv_col,
    kernel,
    near_index,
    near_coef,
):
    p = lax.axis_index("patch").astype(I32)
    own = lax.axis_index("slab").astype(I32) * N_PATCH + p
    meta = jnp.stack([p, own])
    quarter = jnp.asarray(quarter_table())
    x_forward, x_backward = (jnp.asarray(t) for t in x_tables())
    y_forward, y_backward = (jnp.asarray(t) for t in y_tables())
    z_forward, z_backward = (jnp.asarray(t) for t in z_tables())
    charge = density.reshape(4, 128)
    panel, weight, back_weight, row, col = (
        jnp.transpose(a[0]) for a in (send_panel, send_weight, interp_weight, recv_row, recv_col)
    )

    items, message = run_items(charge, counts, panel, weight, row, col)
    message = run_message(exchange(items, "slab"), message)
    data = exchange(message, "patch")
    near = call(near_kernel, (4, 128), [data, near_index, near_coef])

    lines = run_forward(meta, data, quarter, x_forward, y_forward)
    lines = exchange(lines, "slab")

    unit = 2.0 / (NX * NY * NZ)
    alone = (own == 0) | (own == NX // 2)
    below = own < NX // 2
    factor = jnp.stack(
        [
            jnp.where(alone, 0.25 * unit, jnp.where(below, unit, 0.0)),
            jnp.where(alone, 0.25 * unit, jnp.where(below, 0.0, unit)),
            jnp.where(alone, 0.25 * unit, 0.0),
            jnp.where(alone, -0.25 * unit, 0.0),
            jnp.full((), unit, F32),
        ]
    ).astype(F32)
    lines = run_spectrum(factor, kernel, lines, z_forward, z_backward)
    lines = exchange(lines, "slab")
    parts = run_backward(meta, lines, data, quarter, x_backward, y_backward)
    parts = exchange(parts, "patch")
    sampled = call(sum_kernel, (N_SLAB, 1, 64), [parts])
    sampled = exchange(sampled, "slab")
    result = call(interp_kernel, (4, 128), [sampled, counts, panel, back_weight, near])
    return result.reshape(-1)


def solution(mesh):
    placed = (
        P(("slab", "patch")),
        P(("slab", "patch"), None),
        P(("slab", "patch"), None, None),
        P(("slab", "patch"), None, None),
        P(("slab", "patch"), None, None),
        P(("slab", "patch"), None, None),
        P(("slab", "patch"), None, None),
        P(("slab", "patch"), None, None),
        P(None, ("slab", "patch")),
        P(None, ("slab", "patch")),
    )
    return jax.shard_map(
        per_device, mesh=mesh, in_specs=placed, out_specs=P(("slab", "patch")), check_vma=False
    )
```

```python
import math

import jax
import jax.numpy as jnp
import ml_dtypes
import numpy as np
from jax import lax
from jax.experimental import pallas as pl
from jax.experimental.pallas import tpu as pltpu
from jax.sharding import PartitionSpec as P

NX, NY, NZ = 512, 512, 256
N_SLAB, N_PATCH, CAP = 64, 8, 8
DEVICES = N_SLAB * N_PATCH
F32, BF16, I32 = jnp.float32, jnp.bfloat16, jnp.int32
MIB = 1024 * 1024


def halves(table):
    high = table.astype(np.float32).astype(ml_dtypes.bfloat16)
    low = (table - high.astype(np.float64)).astype(np.float32).astype(ml_dtypes.bfloat16)
    return np.stack([high, low])


def wide(table):
    high, low = halves(table)
    return np.concatenate([high, high, low], axis=1)


def waves(first, second, length):
    turns = np.outer(first, second) % length
    angles = turns * (2.0 * np.pi / length)
    cosine, sine = np.cos(angles), np.sin(angles)
    cosine[(4 * turns == length) | (4 * turns == 3 * length)] = 0.0
    sine[(turns == 0) | (2 * turns == length)] = 0.0
    return cosine, sine


def x_tables():
    cosine, sine = waves(np.arange(64), np.arange(64), 64)
    forward = np.block([[cosine, sine], [-sine, cosine]])
    backward = np.block([[cosine, -sine], [sine, cosine]])
    return wide(forward), wide(backward)


def y_tables():
    cosine, sine = waves(np.arange(NY), np.arange(NY // 2), NY)
    sine[:, 0] = 1.0 - 2.0 * (np.arange(NY) % 2)
    return halves(np.concatenate([cosine, sine], axis=1)), halves(np.concatenate([cosine.T, sine.T], axis=0))


def z_tables():
    cosine, sine = waves(np.arange(NZ), np.arange(NZ), NZ)
    depth = NZ // N_SLAB

    def rows(re_part, im_part):
        parts = np.stack([re_part.reshape(N_SLAB, depth, -1), im_part.reshape(N_SLAB, depth, -1)], axis=1)
        return parts.reshape(2 * NZ, -1)

    forward = np.concatenate([rows(cosine, sine), rows(-sine, cosine)], axis=1).T
    backward = np.concatenate([rows(cosine, sine), rows(-sine, cosine)], axis=1)
    return wide(forward), wide(backward)


def quarter_table():
    cosine, sine = waves(np.arange(128), np.ones(1, np.int64), NX)
    return np.stack([cosine[:, 0], sine[:, 0]]).astype(np.float32)


def split(value):
    high = value.astype(BF16)
    return high, (value - high.astype(F32)).astype(BF16)


def mul(a, b):
    return jnp.dot(a, b, preferred_element_type=F32)


def data_by_table(value, table_ref):
    high, low = split(value)
    return mul(high, table_ref[0]) + mul(low, table_ref[0]) + mul(high, table_ref[1])


def wide_by_data(table_ref, value):
    high, low = split(value)
    return mul(table_ref[...], jnp.concatenate([high, low, high], axis=0))


def across(a, b):
    return lax.dot_general(
        a, b, (((1,), (1,)), ((), ())), precision=lax.Precision.HIGHEST, preferred_element_type=F32
    )


def iota(shape, dim):
    return lax.broadcasted_iota(I32, shape, dim)


def spread(values):
    keep = (iota((8, DEVICES), 1) & 7) == iota((8, DEVICES), 0)
    rows = [jnp.where(keep, jnp.broadcast_to(values[c : c + 1, :], (8, DEVICES)), 0.0) for c in range(CAP)]
    return jnp.concatenate(rows, axis=0)


def slab_of():
    return ((iota((N_SLAB, DEVICES), 1) >> 3) == iota((N_SLAB, DEVICES), 0)).astype(F32)


def paired(values):
    rows = [
        jnp.concatenate([values[16 * q : 16 * q + 8, :], values[16 * q + 8 : 16 * q + 16, :]], axis=1)
        for q in range(CAP // 2)
    ]
    return jnp.concatenate(rows, axis=0)


def unpaired(values):
    rows = []
    for q in range(CAP // 2):
        rows.append(values[8 * q : 8 * q + 8, :64])
        rows.append(values[8 * q : 8 * q + 8, 64:])
    return jnp.concatenate(rows, axis=0)


def lookup(row, places):
    return jnp.take_along_axis(
        jnp.broadcast_to(row, places.shape), places, axis=1, mode="promise_in_bounds"
    )


def fetch(sources, held, done):
    copies = [pltpu.make_async_copy(a, b, done.at[k]) for k, (a, b) in enumerate(zip(sources, held))]
    for copy in copies:
        copy.start()
    for copy in copies:
        copy.wait()


def items_kernel(*refs):
    sources, out, held, done = refs[:4], refs[4], refs[5:9], refs[9]
    fetch(sources, held, done)
    density, counts, panel, weight = held
    used = iota((CAP, DEVICES), 0) < counts[...]
    picked = []
    for j in range(4):
        places = panel[:, 128 * j : 128 * (j + 1)]
        low, high = places & 127, places >> 7
        value = jnp.zeros(places.shape, F32)
        for h in range(4):
            value = jnp.where(high == h, lookup(density[h : h + 1, :], low), value)
        picked.append(value)
    items = jnp.where(used, weight[...] * jnp.concatenate(picked, axis=1), 0.0)
    out[:, 0, :] = across(slab_of(), spread(items))


def cells_kernel(density, row, col, out):
    place = (row[...] * NX + col[...]).astype(F32)
    out[0:32, :] = paired(across(spread(place), slab_of()))
    out[32:36, :] = density[...]
    out[36:40, :] = density[...]


def message_kernel(arrived, cells, out):
    items = paired(arrived[:, 0, :].T)
    for p in range(N_PATCH):
        out[p, 0:32, :] = items
        out[p, 32:72, :] = cells[...]


def phases(cell, p, quarter):
    place = (cell + 0.5).astype(I32)
    col = place & (NX - 1)
    turn = (col * p) & (NX - 1)
    part, within = turn >> 7, turn & 127
    cosine, sine = lookup(quarter[0:1, :], within), lookup(quarter[1:2, :], within)
    odd = (part & 1) == 1
    real, imag = jnp.where(odd, sine, cosine), jnp.where(odd, cosine, sine)
    real = jnp.where((part == 1) | (part == 2), -real, real)
    imag = jnp.where(part >= 2, -imag, imag)
    return (place >> 9).astype(F32), (col & 63).astype(F32), real, imag


def lanes(ref, block, p, kind=0):
    rows = [ref[kind, block, 8 * q + p : 8 * q + p + 1, :] for q in range(4)]
    return jnp.concatenate(rows, axis=1)


def thick(row, count):
    return jnp.concatenate([jnp.broadcast_to(row, (16, row.shape[1])).astype(BF16)] * count, axis=0)


def one_hot(row, count, size):
    steps = lax.broadcasted_iota(I32, (size, row.shape[1]), 0).astype(F32).astype(BF16)
    return thick(row, count) == steps


def forward_kernel(meta, data, quarter, x_table, y_table, out, slots, lines):
    p = meta[0]
    for q in range(4):
        for sender in range(N_PATCH):
            slots[4, :, 8 * q + sender, :] = data[sender, 8 * q : 8 * q + 8, :]
    for block in range(N_PATCH):
        row, low_col, cosine, sine = phases(data[block, 32:64, :], p, quarter)
        slots[0, block] = row
        slots[1, block] = low_col
        slots[2, block] = slots[4, block] * cosine
        slots[3, block] = -slots[4, block] * sine

    for block in range(N_PATCH):
        total = jnp.zeros((256, 256), F32)
        for sender in range(N_PATCH):
            in_row = one_hot(lanes(slots, block, sender, 0), 16, 256)
            in_col = one_hot(lanes(slots, block, sender, 1), 4, 64)
            none = jnp.zeros((64, 512), BF16)
            re_high, re_low = split(lanes(slots, block, sender, 2))
            im_high, im_low = split(lanes(slots, block, sender, 3))
            parts = [jnp.where(in_col, thick(v.astype(F32), 4), none) for v in (re_high, im_high, re_low, im_low)]
            ones = jnp.where(in_row, jnp.ones((256, 512), BF16), jnp.zeros((256, 512), BF16))
            total = total + lax.dot_general(
                jnp.concatenate(parts, axis=0),
                ones,
                (((1,), (1,)), ((), ())),
                preferred_element_type=F32,
            )
        lines[block] = total[:128, :] + total[128:, :]
    waved = wide_by_data(x_table, jnp.concatenate([lines[b] for b in range(N_PATCH)], axis=1))
    lower = iota((128, 128), 1) < 64
    rows = []
    for z in range(4):
        tiles = []
        for t in range(4):
            start = 512 * t + 128 * (z // 2)
            even, odd = waved[:, start : start + 128], waved[:, start + 256 : start + 384]
            if z % 2 == 0:
                tiles.append(jnp.where(lower, even, pltpu.roll(odd, 64, 1)))
            else:
                tiles.append(jnp.where(lower, pltpu.roll(even, 64, 1), odd))
        rows.append(jnp.concatenate(tiles, axis=1))
    both = data_by_table(jnp.concatenate(rows, axis=0), y_table)
    kx = 8 * iota((64, 256), 0) + p
    first = iota((64, 256), 1) == 0
    alone = (kx == 0) | (kx == NX // 2)
    for z in range(4):
        real, imag = both[128 * z : 128 * z + 64], both[128 * z + 64 : 128 * z + 128]
        re_cos, re_sin = real[:, :256], real[:, 256:]
        im_cos, im_sin = imag[:, :256], imag[:, 256:]
        re_first = jnp.where(kx <= NX // 2, re_cos, re_sin)
        im_first = jnp.where(alone, re_sin, jnp.where(kx < NX // 2, im_cos, im_sin))
        out[:, z, :] = jnp.where(first, re_first, re_cos + im_sin)
        out[:, 4 + z, :] = jnp.where(first, im_first, im_cos - re_sin)


def spectrum_kernel(factor, kernel, lines, forward, backward, out):
    size = NY // 2
    green = kernel[0, :size, :].T
    base = factor[4]
    low, mid = kernel[0, 0:8, :].T[:, 0:1], kernel[0, size : size + 8, :].T[:, 0:1]
    first = iota((NZ, size), 1) == 0
    own = jnp.where(first, factor[0] * low + factor[1] * mid, base * green)
    mirrored = jnp.where(first[:, :128], factor[2] * low + factor[3] * mid, 0.0)
    value = lines[...].reshape(2 * NZ, size)
    sign = jnp.where((iota((2 * NZ, 128), 0) & 4) == 0, 1.0, -1.0)
    wave = wide_by_data(forward, value)
    turned = wide_by_data(forward, value[:, :128] * sign)
    left = jnp.concatenate([own[:, :128]] * 2, axis=0) * wave[:, :128]
    left = left + jnp.concatenate([mirrored] * 2, axis=0) * turned
    right = jnp.concatenate([own[:, 128:]] * 2, axis=0) * wave[:, 128:]
    scaled = jnp.concatenate([left, right], axis=1)
    out[...] = wide_by_data(backward, scaled).reshape(N_SLAB, 8, size)


def backward_kernel(meta, arrived, data, quarter, x_table, y_table, out, slots, planes, blocks):
    p = meta[0]
    for block in range(N_PATCH):
        row, low_col, cosine, sine = phases(data[block, 32:64, :], p, quarter)
        slots[0, block] = row
        slots[1, block] = low_col
        slots[2, block] = cosine
        slots[3, block] = sine
    value = arrived[...].reshape(512, 256)
    place = iota((512, 256), 0)
    real = (place & 4) == 0
    kx = 8 * (place >> 3) + p
    first = iota((512, 256), 1) == 0
    alone = (kx == 0) | (kx == NX // 2)
    after, before = pltpu.roll(value, 508, 0), pltpu.roll(value, 4, 0)
    keep = (kx <= NX // 2) & (real | ~alone)
    straight = jnp.where(first & ~keep, 0.0, value)
    other = jnp.where(kx > NX // 2, value, jnp.where(alone & real, after, 0.0))
    crossed = jnp.where(first, other, jnp.where(real, -after, before))
    planes[...] = data_by_table(jnp.concatenate([straight, crossed], axis=1), y_table).reshape(64, 8, 512)
    lower = iota((128, 128), 1) < 64
    both = [jnp.concatenate([planes[:, z, :], planes[:, 4 + z, :]], axis=0) for z in range(4)]
    waved = wide_by_data(x_table, jnp.concatenate(both, axis=1))
    for pair in range(2):
        for t in range(4):
            start = 1024 * pair + 128 * t
            even, odd = waved[:, start : start + 128], waved[:, start + 512 : start + 640]
            for block, tile in (
                (2 * t, jnp.where(lower, even, pltpu.roll(odd, 64, 1))),
                (2 * t + 1, jnp.where(lower, pltpu.roll(even, 64, 1), odd)),
            ):
                high, low = split(tile)
                blocks[block, :128, 128 * pair : 128 * (pair + 1)] = high
                blocks[block, 128:, 128 * pair : 128 * (pair + 1)] = low

    steps = iota((64, 512), 0).astype(F32)

    for block in range(N_PATCH):
        field = blocks[block]
        for sender in range(N_PATCH):
            in_row = one_hot(lanes(slots, block, sender, 0), 16, 256)
            ones = jnp.where(in_row, jnp.ones((256, 512), BF16), jnp.zeros((256, 512), BF16))
            near = mul(field, ones)
            re_part = near[0:64] + near[128:192]
            im_part = near[64:128] + near[192:256]
            turned = re_part * lanes(slots, block, sender, 2) - im_part * lanes(slots, block, sender, 3)
            in_col = lanes(slots, block, sender, 1) == steps
            found = jnp.sum(jnp.where(in_col, turned, 0.0), axis=0, keepdims=True)
            for q in range(4):
                out[sender, 8 * q + block : 8 * q + block + 1, :] = found[:, 128 * q : 128 * (q + 1)]


def sum_kernel(parts, out):
    total = parts[0]
    for p in range(1, N_PATCH):
        total = total + parts[p]
    out[:, 0, :] = unpaired(total).T


def near_kernel(data, index, coef, out):
    for j in range(4):
        at = slice(128 * j, 128 * (j + 1))
        total = jnp.zeros((8, 128), F32)
        for half in range(2):
            places = index[8 * half : 8 * half + 8, at]
            low, high = places & 127, places >> 7
            value = jnp.zeros(places.shape, F32)
            for h in range(32):
                value = jnp.where(high == h, lookup(data[h // 4, 64 + h % 4 : 65 + h % 4, :], low), value)
            total = total + coef[8 * half : 8 * half + 8, at] * value
        out[j : j + 1, :] = jnp.sum(total, axis=0, keepdims=True)


def interp_kernel(arrived, counts, panel, weight, near, out):
    used = iota((CAP, DEVICES), 0) < counts[...]
    thin = arrived[:, 0, :].T
    top = thin.astype(BF16)
    middle = (thin - top.astype(F32)).astype(BF16)
    bottom = (thin - top.astype(F32) - middle.astype(F32)).astype(BF16)
    slab = slab_of().astype(BF16)
    expanded = mul(jnp.concatenate([top, middle, bottom], axis=1), jnp.concatenate([slab] * 3, axis=0))
    keep = (iota((64, DEVICES), 1) & 7) == (iota((64, DEVICES), 0) & 7)
    expanded = jnp.where(keep, expanded, 0.0)
    rows = [jnp.sum(expanded[8 * c : 8 * c + 8, :], axis=0, keepdims=True) for c in range(CAP)]
    terms = jnp.where(used, weight[...] * jnp.concatenate(rows, axis=0), 0.0)
    places = panel[...]
    low, high = places & 127, places >> 7
    total = jnp.zeros((16, 128), F32)
    part = iota((16, DEVICES), 0)
    for c in range(CAP):
        term = terms[c : c + 1, :]
        top = term.astype(BF16).astype(F32)
        middle = (term - top).astype(BF16).astype(F32)
        bottom = term - top - middle
        shown = jnp.where(part < 4, top, jnp.where(part < 8, middle, jnp.where(part < 12, bottom, 0.0)))
        left = jnp.where((part & 3) == high[c : c + 1, :], shown, 0.0).astype(BF16)
        right = (iota((128, DEVICES), 0) == low[c : c + 1, :]).astype(F32).astype(BF16)
        total = total + lax.dot_general(left, right, (((1,), (1,)), ((), ())), preferred_element_type=F32)
    out[...] = total[0:4] + total[4:8] + total[8:12] + near[...]


VMEM = pl.BlockSpec(memory_space=pltpu.VMEM)
SMEM = pl.BlockSpec(memory_space=pltpu.SMEM)
FAR = pl.BlockSpec(memory_space=pltpu.HBM)


def call(kernel, shapes, args, scratch=(), scalars=0, vmem=16, sources=None):
    many = isinstance(shapes, list)
    shape = [jax.ShapeDtypeStruct(s, F32) for s in (shapes if many else [shapes])]
    moved = 4 * sum(math.prod(o.shape) for o in shape) + sum(a.size * a.dtype.itemsize for a in args)
    return pl.pallas_call(
        kernel,
        out_shape=shape if many else shape[0],
        in_specs=sources or [SMEM] * scalars + [VMEM] * (len(args) - scalars),
        out_specs=[VMEM] * len(shape) if many else VMEM,
        scratch_shapes=list(scratch),
        compiler_params=pltpu.CompilerParams(vmem_limit_bytes=vmem * MIB),
        cost_estimate=pl.CostEstimate(flops=0, bytes_accessed=moved, transcendentals=0),
    )(*args)


def call_far(kernel, shape, args):
    held = [pltpu.VMEM(a.shape, a.dtype) for a in args]
    done = [pltpu.SemaphoreType.DMA((len(args),))]
    return call(kernel, shape, args, held + done, vmem=60, sources=[FAR] * len(args))


def run_items(density, counts, panel, weight):
    return call_far(items_kernel, (N_SLAB, 1, 64), [density, counts, panel, weight])


def run_cells(density, row, col):
    return call(cells_kernel, (40, 128), [density, row, col])


def run_message(arrived, cells):
    return call(message_kernel, (N_PATCH, 72, 128), [arrived, cells])


def run_sum(parts):
    return call(sum_kernel, (N_SLAB, 1, 64), [parts])


def run_near(data, index, coef):
    return call(near_kernel, (4, 128), [data, index, coef])


def run_interp(*args):
    return call(interp_kernel, (4, 128), list(args))


def exchange(value, axis):
    return lax.all_to_all(value, axis, split_axis=0, concat_axis=0, tiled=True)


def run_forward(meta, data, quarter, x_table, y_table):
    return call(
        forward_kernel,
        (N_SLAB, 8, 256),
        [meta, data, quarter, x_table, y_table],
        [pltpu.VMEM((5, N_PATCH, 32, 128), F32), pltpu.VMEM((N_PATCH, 128, 256), F32)],
        scalars=1,
        vmem=32,
    )


def run_spectrum(factor, kernel, lines, forward, backward):
    return call(
        spectrum_kernel, (N_SLAB, 8, 256), [factor, kernel, lines, forward, backward], scalars=1, vmem=24
    )


def run_backward(meta, lines, data, quarter, x_table, y_table):
    return call(
        backward_kernel,
        (N_PATCH, 32, 128),
        [meta, lines, data, quarter, x_table, y_table],
        [
            pltpu.VMEM((4, N_PATCH, 32, 128), F32),
            pltpu.VMEM((N_SLAB, 8, 512), F32),
            pltpu.VMEM((N_PATCH, 256, 256), BF16),
        ],
        scalars=1,
        vmem=32,
    )


def per_device(
    density,
    counts,
    send_panel,
    send_weight,
    interp_weight,
    recv_row,
    recv_col,
    kernel,
    near_index,
    near_coef,
):
    p = lax.axis_index("patch").astype(I32)
    own = lax.axis_index("slab").astype(I32) * N_PATCH + p
    meta = jnp.stack([p, own])
    quarter = jnp.asarray(quarter_table())
    x_forward, x_backward = (jnp.asarray(t) for t in x_tables())
    y_forward, y_backward = (jnp.asarray(t) for t in y_tables())
    z_forward, z_backward = (jnp.asarray(t) for t in z_tables())
    charge = density.reshape(4, 128)
    panel, weight, back_weight, row, col = (
        jnp.transpose(a[0]) for a in (send_panel, send_weight, interp_weight, recv_row, recv_col)
    )

    unit = 2.0 / (NX * NY * NZ)
    alone = (own == 0) | (own == NX // 2)
    below = own < NX // 2
    factor = jnp.stack(
        [
            jnp.where(alone, 0.25 * unit, jnp.where(below, unit, 0.0)),
            jnp.where(alone, 0.25 * unit, jnp.where(below, 0.0, unit)),
            jnp.where(alone, 0.25 * unit, 0.0),
            jnp.where(alone, -0.25 * unit, 0.0),
            jnp.full((), unit, F32),
        ]
    ).astype(F32)

    items = exchange(run_items(charge, counts, panel, weight), "slab")
    message = run_message(items, run_cells(charge, row, col))
    data = exchange(message, "patch")
    near = run_near(data, near_index, near_coef)

    lines = run_forward(meta, data, quarter, x_forward, y_forward)
    lines = exchange(lines, "slab")

    lines = run_spectrum(factor, kernel, lines, z_forward, z_backward)
    lines = exchange(lines, "slab")
    parts = run_backward(meta, lines, data, quarter, x_backward, y_backward)
    parts = exchange(parts, "patch")
    sampled = run_sum(parts)
    sampled = exchange(sampled, "slab")
    result = run_interp(sampled, counts, panel, back_weight, near)
    return result.reshape(-1)


def solution(mesh):
    placed = (
        P(("slab", "patch")),
        P(("slab", "patch"), None),
        P(("slab", "patch"), None, None),
        P(("slab", "patch"), None, None),
        P(("slab", "patch"), None, None),
        P(("slab", "patch"), None, None),
        P(("slab", "patch"), None, None),
        P(("slab", "patch"), None, None),
        P(None, ("slab", "patch")),
        P(None, ("slab", "patch")),
    )
    return jax.shard_map(
        per_device, mesh=mesh, in_specs=placed, out_specs=P(("slab", "patch")), check_vma=False
    )
```

```python
import math

import jax
import jax.numpy as jnp
import ml_dtypes
import numpy as np
from jax import lax
from jax.experimental import pallas as pl
from jax.experimental.pallas import tpu as pltpu
from jax.sharding import PartitionSpec as P

NX, NY, NZ = 512, 512, 256
N_SLAB, N_PATCH, CAP = 64, 8, 8
DEVICES = N_SLAB * N_PATCH
F32, BF16, I32 = jnp.float32, jnp.bfloat16, jnp.int32
MIB = 1024 * 1024


def halves(table):
    high = table.astype(np.float32).astype(ml_dtypes.bfloat16)
    low = (table - high.astype(np.float64)).astype(np.float32).astype(ml_dtypes.bfloat16)
    return np.stack([high, low])


def wide(table):
    high, low = halves(table)
    return np.concatenate([high, high, low], axis=1)


def waves(first, second, length):
    turns = np.outer(first, second) % length
    angles = turns * (2.0 * np.pi / length)
    cosine, sine = np.cos(angles), np.sin(angles)
    cosine[(4 * turns == length) | (4 * turns == 3 * length)] = 0.0
    sine[(turns == 0) | (2 * turns == length)] = 0.0
    return cosine, sine


def x_tables():
    cosine, sine = waves(np.arange(64), np.arange(64), 64)
    forward = np.block([[cosine, sine], [-sine, cosine]])
    backward = np.block([[cosine, -sine], [sine, cosine]])
    return wide(forward), wide(backward)


def y_tables():
    cosine, sine = waves(np.arange(NY), np.arange(NY // 2), NY)
    sine[:, 0] = 1.0 - 2.0 * (np.arange(NY) % 2)
    return halves(np.concatenate([cosine, sine], axis=1)), halves(np.concatenate([cosine.T, sine.T], axis=0))


def z_tables():
    cosine, sine = waves(np.arange(NZ), np.arange(NZ), NZ)
    depth = NZ // N_SLAB

    def rows(re_part, im_part):
        parts = np.stack([re_part.reshape(N_SLAB, depth, -1), im_part.reshape(N_SLAB, depth, -1)], axis=1)
        return parts.reshape(2 * NZ, -1)

    forward = np.concatenate([rows(cosine, sine), rows(-sine, cosine)], axis=1).T
    backward = np.concatenate([rows(cosine, sine), rows(-sine, cosine)], axis=1)
    return halves(forward), halves(backward)


def quarter_table():
    cosine, sine = waves(np.arange(128), np.ones(1, np.int64), NX)
    return np.stack([cosine[:, 0], sine[:, 0]]).astype(np.float32)


def split(value):
    high = value.astype(BF16)
    return high, (value - high.astype(F32)).astype(BF16)


def mul(a, b):
    return jnp.dot(a, b, preferred_element_type=F32)


def data_by_table(value, table_ref):
    high, low = split(value)
    return mul(high, table_ref[0]) + mul(low, table_ref[0]) + mul(high, table_ref[1])


def table_by_data(table_ref, value):
    high, low = split(value)
    return mul(table_ref[0], high) + mul(table_ref[0], low) + mul(table_ref[1], high)


def wide_by_data(table_ref, value):
    high, low = split(value)
    return mul(table_ref[...], jnp.concatenate([high, low, high], axis=0))


def across(a, b):
    return lax.dot_general(
        a, b, (((1,), (1,)), ((), ())), precision=lax.Precision.HIGHEST, preferred_element_type=F32
    )


def iota(shape, dim):
    return lax.broadcasted_iota(I32, shape, dim)


def spread(values):
    keep = (iota((8, DEVICES), 1) & 7) == iota((8, DEVICES), 0)
    rows = [jnp.where(keep, jnp.broadcast_to(values[c : c + 1, :], (8, DEVICES)), 0.0) for c in range(CAP)]
    return jnp.concatenate(rows, axis=0)


def slab_of():
    return ((iota((N_SLAB, DEVICES), 1) >> 3) == iota((N_SLAB, DEVICES), 0)).astype(F32)


def paired(values):
    rows = [
        jnp.concatenate([values[16 * q : 16 * q + 8, :], values[16 * q + 8 : 16 * q + 16, :]], axis=1)
        for q in range(CAP // 2)
    ]
    return jnp.concatenate(rows, axis=0)


def unpaired(values):
    rows = []
    for q in range(CAP // 2):
        rows.append(values[8 * q : 8 * q + 8, :64])
        rows.append(values[8 * q : 8 * q + 8, 64:])
    return jnp.concatenate(rows, axis=0)


def lookup(row, places):
    return jnp.take_along_axis(
        jnp.broadcast_to(row, places.shape), places, axis=1, mode="promise_in_bounds"
    )


def fetch(sources, held, done):
    copies = [pltpu.make_async_copy(a, b, done.at[k]) for k, (a, b) in enumerate(zip(sources, held))]
    for copy in copies:
        copy.start()
    for copy in copies:
        copy.wait()


def items_kernel(*refs):
    sources, out, held, done = refs[:4], refs[4], refs[5:9], refs[9]
    fetch(sources, held, done)
    density, counts, panel, weight = held
    used = iota((CAP, DEVICES), 0) < counts[...]
    picked = []
    for j in range(4):
        places = panel[:, 128 * j : 128 * (j + 1)]
        low, high = places & 127, places >> 7
        value = jnp.zeros(places.shape, F32)
        for h in range(4):
            value = jnp.where(high == h, lookup(density[h : h + 1, :], low), value)
        picked.append(value)
    items = jnp.where(used, weight[...] * jnp.concatenate(picked, axis=1), 0.0)
    out[:, 0, :] = across(slab_of(), spread(items))


def cells_kernel(density, row, col, out):
    place = (row[...] * NX + col[...]).astype(F32)
    out[0:32, :] = paired(across(spread(place), slab_of()))
    out[32:36, :] = density[...]
    out[36:40, :] = density[...]


def message_kernel(arrived, cells, out):
    items = paired(arrived[:, 0, :].T)
    for p in range(N_PATCH):
        out[p, 0:32, :] = items
        out[p, 32:72, :] = cells[...]


def phases(cell, p, quarter):
    place = (cell + 0.5).astype(I32)
    col = place & (NX - 1)
    turn = (col * p) & (NX - 1)
    part, within = turn >> 7, turn & 127
    cosine, sine = lookup(quarter[0:1, :], within), lookup(quarter[1:2, :], within)
    odd = (part & 1) == 1
    real, imag = jnp.where(odd, sine, cosine), jnp.where(odd, cosine, sine)
    real = jnp.where((part == 1) | (part == 2), -real, real)
    imag = jnp.where(part >= 2, -imag, imag)
    return (place >> 9).astype(F32), (col & 63).astype(F32), real, imag


def lanes(ref, block, p, kind=0):
    rows = [ref[kind, block, 8 * q + p : 8 * q + p + 1, :] for q in range(4)]
    return jnp.concatenate(rows, axis=1)


def thick(row, count):
    return jnp.concatenate([jnp.broadcast_to(row, (16, row.shape[1])).astype(BF16)] * count, axis=0)


def one_hot(row, count, size):
    steps = lax.broadcasted_iota(I32, (size, row.shape[1]), 0).astype(F32).astype(BF16)
    return thick(row, count) == steps


def forward_kernel(meta, data, quarter, x_table, y_table, out, slots, lines):
    p = meta[0]
    for q in range(4):
        for sender in range(N_PATCH):
            slots[4, :, 8 * q + sender, :] = data[sender, 8 * q : 8 * q + 8, :]
    for block in range(N_PATCH):
        row, low_col, cosine, sine = phases(data[block, 32:64, :], p, quarter)
        slots[0, block] = row
        slots[1, block] = low_col
        slots[2, block] = slots[4, block] * cosine
        slots[3, block] = -slots[4, block] * sine

    for block in range(N_PATCH):
        total = jnp.zeros((256, 256), F32)
        for sender in range(N_PATCH):
            in_row = one_hot(lanes(slots, block, sender, 0), 16, 256)
            in_col = one_hot(lanes(slots, block, sender, 1), 4, 64)
            none = jnp.zeros((64, 512), BF16)
            re_high, re_low = split(lanes(slots, block, sender, 2))
            im_high, im_low = split(lanes(slots, block, sender, 3))
            parts = [jnp.where(in_col, thick(v.astype(F32), 4), none) for v in (re_high, im_high, re_low, im_low)]
            ones = jnp.where(in_row, jnp.ones((256, 512), BF16), jnp.zeros((256, 512), BF16))
            total = total + lax.dot_general(
                jnp.concatenate(parts, axis=0),
                ones,
                (((1,), (1,)), ((), ())),
                preferred_element_type=F32,
            )
        lines[block] = total[:128, :] + total[128:, :]
    waved = wide_by_data(x_table, jnp.concatenate([lines[b] for b in range(N_PATCH)], axis=1))
    lower = iota((128, 128), 1) < 64
    rows = []
    for z in range(4):
        tiles = []
        for t in range(4):
            start = 512 * t + 128 * (z // 2)
            even, odd = waved[:, start : start + 128], waved[:, start + 256 : start + 384]
            if z % 2 == 0:
                tiles.append(jnp.where(lower, even, pltpu.roll(odd, 64, 1)))
            else:
                tiles.append(jnp.where(lower, pltpu.roll(even, 64, 1), odd))
        rows.append(jnp.concatenate(tiles, axis=1))
    both = data_by_table(jnp.concatenate(rows, axis=0), y_table)
    kx = 8 * iota((64, 256), 0) + p
    first = iota((64, 256), 1) == 0
    alone = (kx == 0) | (kx == NX // 2)
    for z in range(4):
        real, imag = both[128 * z : 128 * z + 64], both[128 * z + 64 : 128 * z + 128]
        re_cos, re_sin = real[:, :256], real[:, 256:]
        im_cos, im_sin = imag[:, :256], imag[:, 256:]
        re_first = jnp.where(kx <= NX // 2, re_cos, re_sin)
        im_first = jnp.where(alone, re_sin, jnp.where(kx < NX // 2, im_cos, im_sin))
        out[:, z, :] = jnp.where(first, re_first, re_cos + im_sin)
        out[:, 4 + z, :] = jnp.where(first, im_first, im_cos - re_sin)


def spectrum_kernel(factor, kernel, lines, forward, backward, out):
    size = NY // 2
    green = kernel[0, :size, :].T
    base = factor[4]
    low, mid = kernel[0, 0:8, :].T[:, 0:1], kernel[0, size : size + 8, :].T[:, 0:1]
    first = iota((NZ, size), 1) == 0
    own = jnp.where(first, factor[0] * low + factor[1] * mid, base * green)
    mirrored = jnp.where(first[:, :128], factor[2] * low + factor[3] * mid, 0.0)
    value = lines[...].reshape(2 * NZ, size)
    sign = jnp.where((iota((2 * NZ, 128), 0) & 4) == 0, 1.0, -1.0)
    wave = table_by_data(forward, value)
    turned = table_by_data(forward, value[:, :128] * sign)
    left = jnp.concatenate([own[:, :128]] * 2, axis=0) * wave[:, :128]
    left = left + jnp.concatenate([mirrored] * 2, axis=0) * turned
    right = jnp.concatenate([own[:, 128:]] * 2, axis=0) * wave[:, 128:]
    scaled = jnp.concatenate([left, right], axis=1)
    out[...] = table_by_data(backward, scaled).reshape(N_SLAB, 8, size)


def backward_kernel(meta, arrived, data, quarter, x_table, y_table, out, slots, planes, blocks):
    p = meta[0]
    for block in range(N_PATCH):
        row, low_col, cosine, sine = phases(data[block, 32:64, :], p, quarter)
        slots[0, block] = row
        slots[1, block] = low_col
        slots[2, block] = cosine
        slots[3, block] = sine
    value = arrived[...].reshape(512, 256)
    place = iota((512, 256), 0)
    real = (place & 4) == 0
    kx = 8 * (place >> 3) + p
    first = iota((512, 256), 1) == 0
    alone = (kx == 0) | (kx == NX // 2)
    after, before = pltpu.roll(value, 508, 0), pltpu.roll(value, 4, 0)
    keep = (kx <= NX // 2) & (real | ~alone)
    straight = jnp.where(first & ~keep, 0.0, value)
    other = jnp.where(kx > NX // 2, value, jnp.where(alone & real, after, 0.0))
    crossed = jnp.where(first, other, jnp.where(real, -after, before))
    planes[...] = data_by_table(jnp.concatenate([straight, crossed], axis=1), y_table).reshape(64, 8, 512)
    lower = iota((128, 128), 1) < 64
    both = [jnp.concatenate([planes[:, z, :], planes[:, 4 + z, :]], axis=0) for z in range(4)]
    waved = wide_by_data(x_table, jnp.concatenate(both, axis=1))
    for pair in range(2):
        for t in range(4):
            start = 1024 * pair + 128 * t
            even, odd = waved[:, start : start + 128], waved[:, start + 512 : start + 640]
            for block, tile in (
                (2 * t, jnp.where(lower, even, pltpu.roll(odd, 64, 1))),
                (2 * t + 1, jnp.where(lower, pltpu.roll(even, 64, 1), odd)),
            ):
                high, low = split(tile)
                blocks[block, :128, 128 * pair : 128 * (pair + 1)] = high
                blocks[block, 128:, 128 * pair : 128 * (pair + 1)] = low

    steps = iota((64, 512), 0).astype(F32)

    for block in range(N_PATCH):
        field = blocks[block]
        for sender in range(N_PATCH):
            in_row = one_hot(lanes(slots, block, sender, 0), 16, 256)
            ones = jnp.where(in_row, jnp.ones((256, 512), BF16), jnp.zeros((256, 512), BF16))
            near = mul(field, ones)
            re_part = near[0:64] + near[128:192]
            im_part = near[64:128] + near[192:256]
            turned = re_part * lanes(slots, block, sender, 2) - im_part * lanes(slots, block, sender, 3)
            in_col = lanes(slots, block, sender, 1) == steps
            found = jnp.sum(jnp.where(in_col, turned, 0.0), axis=0, keepdims=True)
            for q in range(4):
                out[sender, 8 * q + block : 8 * q + block + 1, :] = found[:, 128 * q : 128 * (q + 1)]


def sum_kernel(parts, out):
    total = parts[0]
    for p in range(1, N_PATCH):
        total = total + parts[p]
    out[:, 0, :] = unpaired(total).T


def near_kernel(data, index, coef, out):
    for j in range(4):
        at = slice(128 * j, 128 * (j + 1))
        total = jnp.zeros((8, 128), F32)
        for half in range(2):
            places = index[8 * half : 8 * half + 8, at]
            low, high = places & 127, places >> 7
            value = jnp.zeros(places.shape, F32)
            for h in range(32):
                value = jnp.where(high == h, lookup(data[h // 4, 64 + h % 4 : 65 + h % 4, :], low), value)
            total = total + coef[8 * half : 8 * half + 8, at] * value
        out[j : j + 1, :] = jnp.sum(total, axis=0, keepdims=True)


def interp_kernel(arrived, counts, panel, weight, near, out):
    used = iota((CAP, DEVICES), 0) < counts[...]
    thin = arrived[:, 0, :].T
    top = thin.astype(BF16)
    middle = (thin - top.astype(F32)).astype(BF16)
    bottom = (thin - top.astype(F32) - middle.astype(F32)).astype(BF16)
    slab = slab_of().astype(BF16)
    expanded = mul(jnp.concatenate([top, middle, bottom], axis=1), jnp.concatenate([slab] * 3, axis=0))
    keep = (iota((64, DEVICES), 1) & 7) == (iota((64, DEVICES), 0) & 7)
    expanded = jnp.where(keep, expanded, 0.0)
    rows = [jnp.sum(expanded[8 * c : 8 * c + 8, :], axis=0, keepdims=True) for c in range(CAP)]
    terms = jnp.where(used, weight[...] * jnp.concatenate(rows, axis=0), 0.0)
    places = panel[...]
    low, high = places & 127, places >> 7
    total = jnp.zeros((16, 128), F32)
    part = iota((16, DEVICES), 0)
    for c in range(CAP):
        term = terms[c : c + 1, :]
        top = term.astype(BF16).astype(F32)
        middle = (term - top).astype(BF16).astype(F32)
        bottom = term - top - middle
        shown = jnp.where(part < 4, top, jnp.where(part < 8, middle, jnp.where(part < 12, bottom, 0.0)))
        left = jnp.where((part & 3) == high[c : c + 1, :], shown, 0.0).astype(BF16)
        right = (iota((128, DEVICES), 0) == low[c : c + 1, :]).astype(F32).astype(BF16)
        total = total + lax.dot_general(left, right, (((1,), (1,)), ((), ())), preferred_element_type=F32)
    out[...] = total[0:4] + total[4:8] + total[8:12] + near[...]


VMEM = pl.BlockSpec(memory_space=pltpu.VMEM)
SMEM = pl.BlockSpec(memory_space=pltpu.SMEM)
FAR = pl.BlockSpec(memory_space=pltpu.HBM)


def call(kernel, shapes, args, scratch=(), scalars=0, vmem=16, sources=None, flops=10**7):
    many = isinstance(shapes, list)
    shape = [jax.ShapeDtypeStruct(s, F32) for s in (shapes if many else [shapes])]
    moved = 4 * sum(math.prod(o.shape) for o in shape) + sum(a.size * a.dtype.itemsize for a in args)
    return pl.pallas_call(
        kernel,
        out_shape=shape if many else shape[0],
        in_specs=sources or [SMEM] * scalars + [VMEM] * (len(args) - scalars),
        out_specs=[VMEM] * len(shape) if many else VMEM,
        scratch_shapes=list(scratch),
        compiler_params=pltpu.CompilerParams(vmem_limit_bytes=vmem * MIB),
        cost_estimate=pl.CostEstimate(flops=flops, bytes_accessed=moved, transcendentals=0),
    )(*args)


def call_far(kernel, shape, args):
    held = [pltpu.VMEM(a.shape, a.dtype) for a in args]
    done = [pltpu.SemaphoreType.DMA((len(args),))]
    return call(kernel, shape, args, held + done, vmem=60, sources=[FAR] * len(args))


def run_items(density, counts, panel, weight):
    return call_far(items_kernel, (N_SLAB, 1, 64), [density, counts, panel, weight])


def run_cells(density, row, col):
    return call(cells_kernel, (40, 128), [density, row, col], flops=10**9)


def run_message(arrived, cells):
    return call(message_kernel, (N_PATCH, 72, 128), [arrived, cells], flops=10**9)


def run_sum(parts):
    return call(sum_kernel, (N_SLAB, 1, 64), [parts])


def run_near(data, index, coef):
    return call(near_kernel, (4, 128), [data, index, coef])


def run_interp(*args):
    return call(interp_kernel, (4, 128), list(args))


def exchange(value, axis):
    return lax.all_to_all(value, axis, split_axis=0, concat_axis=0, tiled=True)


def run_forward(meta, data, quarter, x_table, y_table):
    return call(
        forward_kernel,
        (N_SLAB, 8, 256),
        [meta, data, quarter, x_table, y_table],
        [pltpu.VMEM((5, N_PATCH, 32, 128), F32), pltpu.VMEM((N_PATCH, 128, 256), F32)],
        scalars=1,
        vmem=32,
        flops=6 * 10**9,
    )


def run_spectrum(factor, kernel, lines, forward, backward):
    return call(
        spectrum_kernel, (N_SLAB, 8, 256), [factor, kernel, lines, forward, backward], scalars=1, vmem=24, flops=10**9
    )


def run_backward(meta, lines, data, quarter, x_table, y_table):
    return call(
        backward_kernel,
        (N_PATCH, 32, 128),
        [meta, lines, data, quarter, x_table, y_table],
        [
            pltpu.VMEM((4, N_PATCH, 32, 128), F32),
            pltpu.VMEM((N_SLAB, 8, 512), F32),
            pltpu.VMEM((N_PATCH, 256, 256), BF16),
        ],
        scalars=1,
        vmem=32,
        flops=6 * 10**9,
    )


def per_device(
    density,
    counts,
    send_panel,
    send_weight,
    interp_weight,
    recv_row,
    recv_col,
    kernel,
    near_index,
    near_coef,
):
    p = lax.axis_index("patch").astype(I32)
    own = lax.axis_index("slab").astype(I32) * N_PATCH + p
    meta = jnp.stack([p, own])
    quarter = jnp.asarray(quarter_table())
    x_forward, x_backward = (jnp.asarray(t) for t in x_tables())
    y_forward, y_backward = (jnp.asarray(t) for t in y_tables())
    z_forward, z_backward = (jnp.asarray(t) for t in z_tables())
    charge = density.reshape(4, 128)
    panel, weight, back_weight, row, col = (
        jnp.transpose(a[0]) for a in (send_panel, send_weight, interp_weight, recv_row, recv_col)
    )

    unit = 2.0 / (NX * NY * NZ)
    alone = (own == 0) | (own == NX // 2)
    below = own < NX // 2
    factor = jnp.stack(
        [
            jnp.where(alone, 0.25 * unit, jnp.where(below, unit, 0.0)),
            jnp.where(alone, 0.25 * unit, jnp.where(below, 0.0, unit)),
            jnp.where(alone, 0.25 * unit, 0.0),
            jnp.where(alone, -0.25 * unit, 0.0),
            jnp.full((), unit, F32),
        ]
    ).astype(F32)

    items = exchange(run_items(charge, counts, panel, weight), "slab")
    message = run_message(items, run_cells(charge, row, col))
    data = exchange(message, "patch")
    near = run_near(data, near_index, near_coef)

    lines = run_forward(meta, data, quarter, x_forward, y_forward)
    lines = exchange(lines, "slab")

    lines = run_spectrum(factor, kernel, lines, z_forward, z_backward)
    lines = exchange(lines, "slab")
    parts = run_backward(meta, lines, data, quarter, x_backward, y_backward)
    parts = exchange(parts, "patch")
    sampled = run_sum(parts)
    sampled = exchange(sampled, "slab")
    result = run_interp(sampled, counts, panel, back_weight, near)
    return result.reshape(-1)


def solution(mesh):
    placed = (
        P(("slab", "patch")),
        P(("slab", "patch"), None),
        P(("slab", "patch"), None, None),
        P(("slab", "patch"), None, None),
        P(("slab", "patch"), None, None),
        P(("slab", "patch"), None, None),
        P(("slab", "patch"), None, None),
        P(("slab", "patch"), None, None),
        P(None, ("slab", "patch")),
        P(None, ("slab", "patch")),
    )
    return jax.shard_map(
        per_device, mesh=mesh, in_specs=placed, out_specs=P(("slab", "patch")), check_vma=False
    )
```

```python
import math

import jax
import jax.numpy as jnp
import ml_dtypes
import numpy as np
from jax import lax
from jax.experimental import pallas as pl
from jax.experimental.pallas import tpu as pltpu
from jax.sharding import PartitionSpec as P

NX, NY, NZ = 512, 512, 256
N_SLAB, N_PATCH, CAP = 64, 8, 8
DEVICES = N_SLAB * N_PATCH
F32, BF16, I32 = jnp.float32, jnp.bfloat16, jnp.int32
MIB = 1024 * 1024
GATHERED = (0, 4)


def halves(table):
    high = table.astype(np.float32).astype(ml_dtypes.bfloat16)
    low = (table - high.astype(np.float64)).astype(np.float32).astype(ml_dtypes.bfloat16)
    return np.stack([high, low])


def wide(table):
    high, low = halves(table)
    return np.block([[high, high], [low, np.zeros_like(low)]])


def waves(first, second, length):
    turns = np.outer(first, second) % length
    angles = turns * (2.0 * np.pi / length)
    cosine, sine = np.cos(angles), np.sin(angles)
    cosine[(4 * turns == length) | (4 * turns == 3 * length)] = 0.0
    sine[(turns == 0) | (2 * turns == length)] = 0.0
    return cosine, sine


def x_tables():
    cosine, sine = waves(np.arange(64), np.arange(64), 64)
    forward = np.block([[cosine, sine], [-sine, cosine]])
    backward = np.block([[cosine, -sine], [sine, cosine]])
    return wide(forward), wide(backward)


def y_tables():
    cosine, sine = waves(np.arange(NY), np.arange(NY // 2), NY)
    sine[:, 0] = 1.0 - 2.0 * (np.arange(NY) % 2)
    return halves(np.concatenate([cosine, sine], axis=1)), halves(np.concatenate([cosine.T, sine.T], axis=0))


def z_tables():
    cosine, sine = waves(np.arange(NZ), np.arange(NZ), NZ)
    depth = NZ // N_SLAB

    def rows(re_part, im_part):
        parts = np.stack([re_part.reshape(N_SLAB, depth, -1), im_part.reshape(N_SLAB, depth, -1)], axis=1)
        return parts.reshape(2 * NZ, -1)

    forward = np.concatenate([rows(cosine, sine), rows(-sine, cosine)], axis=1).T
    backward = np.concatenate([rows(cosine, sine), rows(-sine, cosine)], axis=1)
    return halves(forward), halves(backward)


def quarter_table():
    cosine, sine = waves(np.arange(128), np.ones(1, np.int64), NX)
    return np.stack([cosine[:, 0], sine[:, 0]]).astype(np.float32)


def split(value):
    high = value.astype(BF16)
    return high, (value - high.astype(F32)).astype(BF16)


def mul(a, b):
    return jnp.dot(a, b, preferred_element_type=F32)


def data_by_table(value, table_ref):
    high, low = split(value)
    return mul(high, table_ref[0]) + mul(low, table_ref[0]) + mul(high, table_ref[1])


def table_by_data(table_ref, value):
    high, low = split(value)
    return mul(table_ref[0], high) + mul(table_ref[0], low) + mul(table_ref[1], high)


def wide_by_data(table_ref, value):
    both = mul(table_ref[...], jnp.concatenate(split(value), axis=0))
    return both[:128] + both[128:]


def thirds(value):
    top = value.astype(BF16)
    rest = value - top.astype(F32)
    middle = rest.astype(BF16)
    return [top, middle, (rest - middle.astype(F32)).astype(BF16)]


def across(a, b):
    return lax.dot_general(a, b, (((1,), (1,)), ((), ())), preferred_element_type=F32)


def iota(shape, dim):
    return lax.broadcasted_iota(I32, shape, dim)


def spread(values):
    keep = (iota((8, DEVICES), 1) & 7) == iota((8, DEVICES), 0)
    rows = [jnp.where(keep, jnp.broadcast_to(values[c : c + 1, :], (8, DEVICES)), 0.0) for c in range(CAP)]
    return jnp.concatenate(rows, axis=0)


def slab_of():
    return ((iota((N_SLAB, DEVICES), 1) >> 3) == iota((N_SLAB, DEVICES), 0)).astype(F32).astype(BF16)


def paired(values):
    rows = [
        jnp.concatenate([values[16 * q : 16 * q + 8, :], values[16 * q + 8 : 16 * q + 16, :]], axis=1)
        for q in range(CAP // 2)
    ]
    return jnp.concatenate(rows, axis=0)


def unpaired(values):
    rows = []
    for q in range(CAP // 2):
        rows.append(values[8 * q : 8 * q + 8, :64])
        rows.append(values[8 * q : 8 * q + 8, 64:])
    return jnp.concatenate(rows, axis=0)


def lookup(row, places):
    return jnp.take_along_axis(
        jnp.broadcast_to(row, places.shape), places, axis=1, mode="promise_in_bounds"
    )


def fetch(sources, held, done):
    copies = [pltpu.make_async_copy(a, b, done.at[k]) for k, (a, b) in enumerate(zip(sources, held))]
    for copy in copies:
        copy.start()
    for copy in copies:
        copy.wait()


def items_kernel(*refs):
    sources, out, held, done = refs[:4], refs[4], refs[5:9], refs[9]
    slab = slab_of()
    fetch(sources, held, done)
    density, counts, panel, weight = held
    used = iota((CAP, DEVICES), 0) < counts[...]
    picked = []
    for j in range(4):
        places = panel[:, 128 * j : 128 * (j + 1)]
        low, high = places & 127, places >> 7
        value = jnp.zeros(places.shape, F32)
        for h in range(4):
            value = jnp.where(high == h, lookup(density[h : h + 1, :], low), value)
        picked.append(value)
    items = jnp.where(used, weight[...] * jnp.concatenate(picked, axis=1), 0.0)
    parts = across(slab, jnp.concatenate(thirds(spread(items)), axis=0))
    out[:, 0, :] = parts[:, :64] + parts[:, 64:128] + parts[:, 128:]


def cells_kernel(density, row, col, out):
    place = (row[...] * NX + col[...]).astype(F32)
    parts = across(jnp.concatenate(thirds(spread(place)), axis=0), slab_of())
    out[0:32, :] = paired(parts[:64] + parts[64:128] + parts[128:])
    out[32:36, :] = density[...]
    out[36:40, :] = density[...]


def message_kernel(arrived, cells, out):
    items = paired(arrived[:, 0, :].T)
    for p in range(N_PATCH):
        out[p, 0:32, :] = items
        out[p, 32:72, :] = cells[...]


def phases(cell, p, quarter):
    place = (cell + 0.5).astype(I32)
    col = place & (NX - 1)
    turn = (col * p) & (NX - 1)
    part, within = turn >> 7, turn & 127
    cosine, sine = lookup(quarter[0:1, :], within), lookup(quarter[1:2, :], within)
    odd = (part & 1) == 1
    real, imag = jnp.where(odd, sine, cosine), jnp.where(odd, cosine, sine)
    real = jnp.where((part == 1) | (part == 2), -real, real)
    imag = jnp.where(part >= 2, -imag, imag)
    return (place >> 9).astype(F32), (col & 63).astype(F32), real, imag


def lanes(ref, block, p, kind=0):
    rows = [ref[kind, block, 8 * q + p : 8 * q + p + 1, :] for q in range(4)]
    return jnp.concatenate(rows, axis=1)


def thick(row, count):
    return jnp.concatenate([jnp.broadcast_to(row, (16, row.shape[1])).astype(BF16)] * count, axis=0)


def one_hot(row, count, size):
    steps = lax.broadcasted_iota(I32, (size, row.shape[1]), 0).astype(F32).astype(BF16)
    return thick(row, count) == steps


def forward_kernel(meta, data, quarter, x_table, y_table, out, slots, lines):
    p = meta[0]
    for q in range(4):
        for sender in range(N_PATCH):
            slots[4, :, 8 * q + sender, :] = data[sender, 8 * q : 8 * q + 8, :]
    for block in range(N_PATCH):
        row, low_col, cosine, sine = phases(data[block, 32:64, :], p, quarter)
        slots[0, block] = row
        slots[1, block] = low_col
        slots[2, block] = slots[4, block] * cosine
        slots[3, block] = -slots[4, block] * sine

    for block in range(N_PATCH):
        total = jnp.zeros((256, 256), F32)
        for sender in range(N_PATCH):
            in_row = one_hot(lanes(slots, block, sender, 0), 16, 256)
            in_col = one_hot(lanes(slots, block, sender, 1), 4, 64)
            none = jnp.zeros((64, 512), BF16)
            re_high, re_low = split(lanes(slots, block, sender, 2))
            im_high, im_low = split(lanes(slots, block, sender, 3))
            parts = [jnp.where(in_col, thick(v.astype(F32), 4), none) for v in (re_high, im_high, re_low, im_low)]
            ones = jnp.where(in_row, jnp.ones((256, 512), BF16), jnp.zeros((256, 512), BF16))
            total = total + lax.dot_general(
                jnp.concatenate(parts, axis=0),
                ones,
                (((1,), (1,)), ((), ())),
                preferred_element_type=F32,
            )
        lines[block] = total[:128, :] + total[128:, :]
    waved = wide_by_data(x_table, jnp.concatenate([lines[b] for b in range(N_PATCH)], axis=1))
    lower = iota((128, 128), 1) < 64
    rows = []
    for z in range(4):
        tiles = []
        for t in range(4):
            start = 512 * t + 128 * (z // 2)
            even, odd = waved[:, start : start + 128], waved[:, start + 256 : start + 384]
            if z % 2 == 0:
                tiles.append(jnp.where(lower, even, pltpu.roll(odd, 64, 1)))
            else:
                tiles.append(jnp.where(lower, pltpu.roll(even, 64, 1), odd))
        rows.append(jnp.concatenate(tiles, axis=1))
    both = data_by_table(jnp.concatenate(rows, axis=0), y_table)
    kx = 8 * iota((64, 256), 0) + p
    first = iota((64, 256), 1) == 0
    alone = (kx == 0) | (kx == NX // 2)
    for z in range(4):
        real, imag = both[128 * z : 128 * z + 64], both[128 * z + 64 : 128 * z + 128]
        re_cos, re_sin = real[:, :256], real[:, 256:]
        im_cos, im_sin = imag[:, :256], imag[:, 256:]
        re_first = jnp.where(kx <= NX // 2, re_cos, re_sin)
        im_first = jnp.where(alone, re_sin, jnp.where(kx < NX // 2, im_cos, im_sin))
        out[:, z, :] = jnp.where(first, re_first, re_cos + im_sin)
        out[:, 4 + z, :] = jnp.where(first, im_first, im_cos - re_sin)


def spectrum_kernel(factor, kernel, lines, forward, backward, out):
    size = NY // 2
    green = kernel[0, :size, :].T
    base = factor[4]
    low, mid = kernel[0, 0:8, :].T[:, 0:1], kernel[0, size : size + 8, :].T[:, 0:1]
    first = iota((NZ, size), 1) == 0
    own = jnp.where(first, factor[0] * low + factor[1] * mid, base * green)
    mirrored = jnp.where(first[:, :128], factor[2] * low + factor[3] * mid, 0.0)
    value = lines[...].reshape(2 * NZ, size)
    sign = jnp.where((iota((2 * NZ, 128), 0) & 4) == 0, 1.0, -1.0)
    wave = table_by_data(forward, value)
    turned = table_by_data(forward, value[:, :128] * sign)
    left = jnp.concatenate([own[:, :128]] * 2, axis=0) * wave[:, :128]
    left = left + jnp.concatenate([mirrored] * 2, axis=0) * turned
    right = jnp.concatenate([own[:, 128:]] * 2, axis=0) * wave[:, 128:]
    scaled = jnp.concatenate([left, right], axis=1)
    out[...] = table_by_data(backward, scaled).reshape(N_SLAB, 8, size)


def gathered(whole, block, slot):
    row, low_col, cosine, sine = (jnp.broadcast_to(v, (8, 128)) for v in slot)
    row = row.astype(I32)
    low, upper = row & 127, row >= 128
    step = iota((8, 128), 0).astype(F32)
    total = jnp.zeros((8, 128), F32)
    for group in range(8):
        part = []
        for kind in range(2):
            at = slice(64 * kind + 8 * group, 64 * kind + 8 * group + 8)
            near = jnp.take_along_axis(whole[block, at, :128], low, axis=1, mode="promise_in_bounds")
            far = jnp.take_along_axis(whole[block, at, 128:], low, axis=1, mode="promise_in_bounds")
            part.append(jnp.where(upper, far, near))
        turned = part[0] * cosine - part[1] * sine
        total = total + jnp.where(low_col == step + 8.0 * group, turned, 0.0)
    return jnp.sum(total, axis=0, keepdims=True)


def backward_kernel(meta, arrived, data, quarter, x_table, y_table, out, slots, planes, blocks, whole):
    p = meta[0]
    for block in range(N_PATCH):
        row, low_col, cosine, sine = phases(data[block, 32:64, :], p, quarter)
        slots[0, block] = row
        slots[1, block] = low_col
        slots[2, block] = cosine
        slots[3, block] = sine
    value = arrived[...].reshape(512, 256)
    place = iota((512, 256), 0)
    real = (place & 4) == 0
    kx = 8 * (place >> 3) + p
    first = iota((512, 256), 1) == 0
    alone = (kx == 0) | (kx == NX // 2)
    after, before = pltpu.roll(value, 508, 0), pltpu.roll(value, 4, 0)
    keep = (kx <= NX // 2) & (real | ~alone)
    straight = jnp.where(first & ~keep, 0.0, value)
    other = jnp.where(kx > NX // 2, value, jnp.where(alone & real, after, 0.0))
    crossed = jnp.where(first, other, jnp.where(real, -after, before))
    planes[...] = data_by_table(jnp.concatenate([straight, crossed], axis=1), y_table).reshape(64, 8, 512)
    lower = iota((128, 128), 1) < 64
    both = [jnp.concatenate([planes[:, z, :], planes[:, 4 + z, :]], axis=0) for z in range(4)]
    waved = wide_by_data(x_table, jnp.concatenate(both, axis=1))
    for pair in range(2):
        for t in range(4):
            start = 1024 * pair + 128 * t
            even, odd = waved[:, start : start + 128], waved[:, start + 512 : start + 640]
            for block, tile in (
                (2 * t, jnp.where(lower, even, pltpu.roll(odd, 64, 1))),
                (2 * t + 1, jnp.where(lower, pltpu.roll(even, 64, 1), odd)),
            ):
                whole[block, :, 128 * pair : 128 * (pair + 1)] = tile
                high, low = split(tile)
                blocks[block, :128, 128 * pair : 128 * (pair + 1)] = high
                blocks[block, 128:, 128 * pair : 128 * (pair + 1)] = low

    steps = iota((64, 512), 0).astype(F32)

    for block in range(N_PATCH):
        field = blocks[block]
        for sender in range(N_PATCH):
            if sender in GATHERED:
                for q in range(4):
                    at = slice(8 * q + sender, 8 * q + sender + 1)
                    out[sender, 8 * q + block : 8 * q + block + 1, :] = gathered(
                        whole, block, [slots[k, block, at, :] for k in range(4)]
                    )
                continue
            in_row = one_hot(lanes(slots, block, sender, 0), 16, 256)
            ones = jnp.where(in_row, jnp.ones((256, 512), BF16), jnp.zeros((256, 512), BF16))
            near = mul(field, ones)
            re_part = near[0:64] + near[128:192]
            im_part = near[64:128] + near[192:256]
            turned = re_part * lanes(slots, block, sender, 2) - im_part * lanes(slots, block, sender, 3)
            in_col = lanes(slots, block, sender, 1) == steps
            found = jnp.sum(jnp.where(in_col, turned, 0.0), axis=0, keepdims=True)
            for q in range(4):
                out[sender, 8 * q + block : 8 * q + block + 1, :] = found[:, 128 * q : 128 * (q + 1)]


def sum_kernel(parts, out):
    total = parts[0]
    for p in range(1, N_PATCH):
        total = total + parts[p]
    out[:, 0, :] = unpaired(total).T


def near_kernel(data, index, coef, out):
    for j in range(4):
        at = slice(128 * j, 128 * (j + 1))
        total = jnp.zeros((8, 128), F32)
        for half in range(2):
            places = index[8 * half : 8 * half + 8, at]
            low, high = places & 127, places >> 7
            value = jnp.zeros(places.shape, F32)
            for h in range(32):
                value = jnp.where(high == h, lookup(data[h // 4, 64 + h % 4 : 65 + h % 4, :], low), value)
            total = total + coef[8 * half : 8 * half + 8, at] * value
        out[j : j + 1, :] = jnp.sum(total, axis=0, keepdims=True)


def interp_kernel(arrived, counts, panel, weight, near, out):
    used = iota((CAP, DEVICES), 0) < counts[...]
    thin = jnp.concatenate(thirds(arrived[:, 0, :].T), axis=1)
    expanded = mul(thin, jnp.concatenate([slab_of()] * 3, axis=0))
    keep = (iota((64, DEVICES), 1) & 7) == (iota((64, DEVICES), 0) & 7)
    expanded = jnp.where(keep, expanded, 0.0)
    rows = [jnp.sum(expanded[8 * c : 8 * c + 8, :], axis=0, keepdims=True) for c in range(CAP)]
    terms = jnp.where(used, weight[...] * jnp.concatenate(rows, axis=0), 0.0)
    places = panel[...]
    low, high = places & 127, places >> 7
    total = jnp.zeros((16, 128), F32)
    part = iota((16, DEVICES), 0)
    for c in range(CAP):
        term = terms[c : c + 1, :]
        top = term.astype(BF16).astype(F32)
        middle = (term - top).astype(BF16).astype(F32)
        bottom = term - top - middle
        shown = jnp.where(part < 4, top, jnp.where(part < 8, middle, jnp.where(part < 12, bottom, 0.0)))
        left = jnp.where((part & 3) == high[c : c + 1, :], shown, 0.0).astype(BF16)
        right = (iota((128, DEVICES), 0) == low[c : c + 1, :]).astype(F32).astype(BF16)
        total = total + lax.dot_general(left, right, (((1,), (1,)), ((), ())), preferred_element_type=F32)
    out[...] = total[0:4] + total[4:8] + total[8:12] + near[...]


VMEM = pl.BlockSpec(memory_space=pltpu.VMEM)
SMEM = pl.BlockSpec(memory_space=pltpu.SMEM)
FAR = pl.BlockSpec(memory_space=pltpu.HBM)


def call(kernel, shapes, args, scratch=(), scalars=0, vmem=16, sources=None, flops=10**7):
    many = isinstance(shapes, list)
    shape = [jax.ShapeDtypeStruct(s, F32) for s in (shapes if many else [shapes])]
    moved = 4 * sum(math.prod(o.shape) for o in shape) + sum(a.size * a.dtype.itemsize for a in args)
    return pl.pallas_call(
        kernel,
        out_shape=shape if many else shape[0],
        in_specs=sources or [SMEM] * scalars + [VMEM] * (len(args) - scalars),
        out_specs=[VMEM] * len(shape) if many else VMEM,
        scratch_shapes=list(scratch),
        compiler_params=pltpu.CompilerParams(vmem_limit_bytes=vmem * MIB),
        cost_estimate=pl.CostEstimate(flops=flops, bytes_accessed=moved, transcendentals=0),
    )(*args)


def call_far(kernel, shape, args):
    held = [pltpu.VMEM(a.shape, a.dtype) for a in args]
    done = [pltpu.SemaphoreType.DMA((len(args),))]
    return call(kernel, shape, args, held + done, vmem=60, sources=[FAR] * len(args))


def run_items(density, counts, panel, weight):
    return call_far(items_kernel, (N_SLAB, 1, 64), [density, counts, panel, weight])


def run_cells(density, row, col):
    return call(cells_kernel, (40, 128), [density, row, col], flops=10**9)


def run_message(arrived, cells):
    return call(message_kernel, (N_PATCH, 72, 128), [arrived, cells], flops=10**9)


def run_sum(parts):
    return call(sum_kernel, (N_SLAB, 1, 64), [parts])


def run_near(data, index, coef):
    return call(near_kernel, (4, 128), [data, index, coef])


def run_interp(*args):
    return call(interp_kernel, (4, 128), list(args))


def exchange(value, axis):
    return lax.all_to_all(value, axis, split_axis=0, concat_axis=0, tiled=True)


def run_forward(meta, data, quarter, x_table, y_table):
    return call(
        forward_kernel,
        (N_SLAB, 8, 256),
        [meta, data, quarter, x_table, y_table],
        [pltpu.VMEM((5, N_PATCH, 32, 128), F32), pltpu.VMEM((N_PATCH, 128, 256), F32)],
        scalars=1,
        vmem=32,
        flops=6 * 10**9,
    )


def run_spectrum(factor, kernel, lines, forward, backward):
    return call(
        spectrum_kernel, (N_SLAB, 8, 256), [factor, kernel, lines, forward, backward], scalars=1, vmem=24, flops=10**9
    )


def run_backward(meta, lines, data, quarter, x_table, y_table):
    return call(
        backward_kernel,
        (N_PATCH, 32, 128),
        [meta, lines, data, quarter, x_table, y_table],
        [
            pltpu.VMEM((4, N_PATCH, 32, 128), F32),
            pltpu.VMEM((N_SLAB, 8, 512), F32),
            pltpu.VMEM((N_PATCH, 256, 256), BF16),
            pltpu.VMEM((N_PATCH, 128, 256), F32),
        ],
        scalars=1,
        vmem=32,
        flops=6 * 10**9,
    )


def per_device(
    density,
    counts,
    send_panel,
    send_weight,
    interp_weight,
    recv_row,
    recv_col,
    kernel,
    near_index,
    near_coef,
):
    p = lax.axis_index("patch").astype(I32)
    own = lax.axis_index("slab").astype(I32) * N_PATCH + p
    meta = jnp.stack([p, own])
    quarter = jnp.asarray(quarter_table())
    x_forward, x_backward = (jnp.asarray(t) for t in x_tables())
    y_forward, y_backward = (jnp.asarray(t) for t in y_tables())
    z_forward, z_backward = (jnp.asarray(t) for t in z_tables())
    charge = density.reshape(4, 128)
    panel, weight, back_weight, row, col = (
        jnp.transpose(a[0]) for a in (send_panel, send_weight, interp_weight, recv_row, recv_col)
    )

    unit = 2.0 / (NX * NY * NZ)
    alone = (own == 0) | (own == NX // 2)
    below = own < NX // 2
    factor = jnp.stack(
        [
            jnp.where(alone, 0.25 * unit, jnp.where(below, unit, 0.0)),
            jnp.where(alone, 0.25 * unit, jnp.where(below, 0.0, unit)),
            jnp.where(alone, 0.25 * unit, 0.0),
            jnp.where(alone, -0.25 * unit, 0.0),
            jnp.full((), unit, F32),
        ]
    ).astype(F32)

    items = exchange(run_items(charge, counts, panel, weight), "slab")
    message = run_message(items, run_cells(charge, row, col))
    data = exchange(message, "patch")
    near = run_near(data, near_index, near_coef)

    lines = run_forward(meta, data, quarter, x_forward, y_forward)
    lines = exchange(lines, "slab")

    lines = run_spectrum(factor, kernel, lines, z_forward, z_backward)
    lines = exchange(lines, "slab")
    parts = run_backward(meta, lines, data, quarter, x_backward, y_backward)
    parts = exchange(parts, "patch")
    sampled = run_sum(parts)
    sampled = exchange(sampled, "slab")
    result = run_interp(sampled, counts, panel, back_weight, near)
    return result.reshape(-1)


def solution(mesh):
    placed = (
        P(("slab", "patch")),
        P(("slab", "patch"), None),
        P(("slab", "patch"), None, None),
        P(("slab", "patch"), None, None),
        P(("slab", "patch"), None, None),
        P(("slab", "patch"), None, None),
        P(("slab", "patch"), None, None),
        P(("slab", "patch"), None, None),
        P(None, ("slab", "patch")),
        P(None, ("slab", "patch")),
    )
    return jax.shard_map(
        per_device, mesh=mesh, in_specs=placed, out_specs=P(("slab", "patch")), check_vma=False
    )
```

```python
import math

import jax
import jax.numpy as jnp
import ml_dtypes
import numpy as np
from jax import lax
from jax.experimental import pallas as pl
from jax.experimental.pallas import tpu as pltpu
from jax.sharding import PartitionSpec as P

NX, NY, NZ = 512, 512, 256
N_SLAB, N_PATCH, CAP = 64, 8, 8
DEVICES = N_SLAB * N_PATCH
F32, BF16, I32 = jnp.float32, jnp.bfloat16, jnp.int32
MIB = 1024 * 1024
GATHERED = (0, 4)


def halves(table):
    high = table.astype(np.float32).astype(ml_dtypes.bfloat16)
    low = (table - high.astype(np.float64)).astype(np.float32).astype(ml_dtypes.bfloat16)
    return np.stack([high, low])


def wide(table):
    high, low = halves(table)
    return np.concatenate([high, high, low], axis=1)


def waves(first, second, length):
    turns = np.outer(first, second) % length
    angles = turns * (2.0 * np.pi / length)
    cosine, sine = np.cos(angles), np.sin(angles)
    cosine[(4 * turns == length) | (4 * turns == 3 * length)] = 0.0
    sine[(turns == 0) | (2 * turns == length)] = 0.0
    return cosine, sine


def x_tables():
    cosine, sine = waves(np.arange(64), np.arange(64), 64)
    forward = np.block([[cosine, sine], [-sine, cosine]])
    backward = np.block([[cosine, -sine], [sine, cosine]])
    return wide(forward), wide(backward)


def y_tables():
    cosine, sine = waves(np.arange(NY), np.arange(NY // 2), NY)
    sine[:, 0] = 1.0 - 2.0 * (np.arange(NY) % 2)
    return halves(np.concatenate([cosine, sine], axis=1)), halves(np.concatenate([cosine.T, sine.T], axis=0))


def z_tables():
    cosine, sine = waves(np.arange(NZ), np.arange(NZ), NZ)
    depth = NZ // N_SLAB

    def rows(re_part, im_part):
        parts = np.stack([re_part.reshape(N_SLAB, depth, -1), im_part.reshape(N_SLAB, depth, -1)], axis=1)
        return parts.reshape(2 * NZ, -1)

    forward = np.concatenate([rows(cosine, sine), rows(-sine, cosine)], axis=1).T
    backward = np.concatenate([rows(cosine, sine), rows(-sine, cosine)], axis=1)
    return halves(forward), halves(backward)


def quarter_table():
    cosine, sine = waves(np.arange(128), np.ones(1, np.int64), NX)
    return np.stack([cosine[:, 0], sine[:, 0]]).astype(np.float32)


def split(value):
    high = value.astype(BF16)
    return high, (value - high.astype(F32)).astype(BF16)


def mul(a, b):
    return jnp.dot(a, b, preferred_element_type=F32)


def data_by_table(value, table_ref):
    high, low = split(value)
    return mul(high, table_ref[0]) + mul(low, table_ref[0]) + mul(high, table_ref[1])


def table_by_data(table_ref, value):
    high, low = split(value)
    return mul(table_ref[0], high) + mul(table_ref[0], low) + mul(table_ref[1], high)


def wide_by_data(table_ref, value):
    high, low = split(value)
    return mul(table_ref[...], jnp.concatenate([high, low, high], axis=0))


def thirds(value):
    top = value.astype(BF16)
    rest = value - top.astype(F32)
    middle = rest.astype(BF16)
    return [top, middle, (rest - middle.astype(F32)).astype(BF16)]


def across(a, b):
    return lax.dot_general(a, b, (((1,), (1,)), ((), ())), preferred_element_type=F32)


def iota(shape, dim):
    return lax.broadcasted_iota(I32, shape, dim)


def spread(values):
    keep = (iota((8, DEVICES), 1) & 7) == iota((8, DEVICES), 0)
    rows = [jnp.where(keep, jnp.broadcast_to(values[c : c + 1, :], (8, DEVICES)), 0.0) for c in range(CAP)]
    return jnp.concatenate(rows, axis=0)


def slab_of():
    return ((iota((N_SLAB, DEVICES), 1) >> 3) == iota((N_SLAB, DEVICES), 0)).astype(F32).astype(BF16)


def paired(values):
    rows = [
        jnp.concatenate([values[16 * q : 16 * q + 8, :], values[16 * q + 8 : 16 * q + 16, :]], axis=1)
        for q in range(CAP // 2)
    ]
    return jnp.concatenate(rows, axis=0)


def unpaired(values):
    rows = []
    for q in range(CAP // 2):
        rows.append(values[8 * q : 8 * q + 8, :64])
        rows.append(values[8 * q : 8 * q + 8, 64:])
    return jnp.concatenate(rows, axis=0)


def lookup(row, places):
    return jnp.take_along_axis(
        jnp.broadcast_to(row, places.shape), places, axis=1, mode="promise_in_bounds"
    )


def fetch(sources, held, done):
    copies = [pltpu.make_async_copy(a, b, done.at[k]) for k, (a, b) in enumerate(zip(sources, held))]
    for copy in copies:
        copy.start()
    for copy in copies:
        copy.wait()


def items_kernel(*refs):
    sources, out, held, done = refs[:4], refs[4], refs[5:9], refs[9]
    slab = slab_of()
    fetch(sources, held, done)
    density, counts, panel, weight = held
    used = iota((CAP, DEVICES), 0) < counts[...]
    picked = []
    for j in range(4):
        places = panel[:, 128 * j : 128 * (j + 1)]
        low, high = places & 127, places >> 7
        value = jnp.zeros(places.shape, F32)
        for h in range(4):
            value = jnp.where(high == h, lookup(density[h : h + 1, :], low), value)
        picked.append(value)
    items = jnp.where(used, weight[...] * jnp.concatenate(picked, axis=1), 0.0)
    parts = across(slab, jnp.concatenate(thirds(spread(items)), axis=0))
    out[:, 0, :] = parts[:, :64] + parts[:, 64:128] + parts[:, 128:]


def cells_kernel(density, row, col, out):
    place = (row[...] * NX + col[...]).astype(F32)
    parts = across(jnp.concatenate(thirds(spread(place)), axis=0), slab_of())
    out[0:32, :] = paired(parts[:64] + parts[64:128] + parts[128:])
    out[32:36, :] = density[...]
    out[36:40, :] = density[...]


def message_kernel(arrived, cells, out):
    items = paired(arrived[:, 0, :].T)
    for p in range(N_PATCH):
        out[p, 0:32, :] = items
        out[p, 32:72, :] = cells[...]


def phases(cell, p, quarter):
    place = (cell + 0.5).astype(I32)
    col = place & (NX - 1)
    turn = (col * p) & (NX - 1)
    part, within = turn >> 7, turn & 127
    cosine, sine = lookup(quarter[0:1, :], within), lookup(quarter[1:2, :], within)
    odd = (part & 1) == 1
    real, imag = jnp.where(odd, sine, cosine), jnp.where(odd, cosine, sine)
    real = jnp.where((part == 1) | (part == 2), -real, real)
    imag = jnp.where(part >= 2, -imag, imag)
    return (place >> 9).astype(F32), (col & 63).astype(F32), real, imag


def lanes(ref, block, p, kind=0):
    rows = [ref[kind, block, 8 * q + p : 8 * q + p + 1, :] for q in range(4)]
    return jnp.concatenate(rows, axis=1)


def thick(row, count):
    return jnp.concatenate([jnp.broadcast_to(row, (16, row.shape[1])).astype(BF16)] * count, axis=0)


def one_hot(row, count, size):
    steps = lax.broadcasted_iota(I32, (size, row.shape[1]), 0).astype(F32).astype(BF16)
    return thick(row, count) == steps


def forward_kernel(meta, data, quarter, x_table, y_table, out, slots, lines):
    p = meta[0]
    for q in range(4):
        for sender in range(N_PATCH):
            slots[4, :, 8 * q + sender, :] = data[sender, 8 * q : 8 * q + 8, :]
    for block in range(N_PATCH):
        row, low_col, cosine, sine = phases(data[block, 32:64, :], p, quarter)
        slots[0, block] = row
        slots[1, block] = low_col
        slots[2, block] = slots[4, block] * cosine
        slots[3, block] = -slots[4, block] * sine

    for block in range(N_PATCH):
        total = jnp.zeros((256, 256), F32)
        for sender in range(N_PATCH):
            in_row = one_hot(lanes(slots, block, sender, 0), 16, 256)
            in_col = one_hot(lanes(slots, block, sender, 1), 4, 64)
            none = jnp.zeros((64, 512), BF16)
            re_high, re_low = split(lanes(slots, block, sender, 2))
            im_high, im_low = split(lanes(slots, block, sender, 3))
            parts = [jnp.where(in_col, thick(v.astype(F32), 4), none) for v in (re_high, im_high, re_low, im_low)]
            ones = jnp.where(in_row, jnp.ones((256, 512), BF16), jnp.zeros((256, 512), BF16))
            total = total + lax.dot_general(
                jnp.concatenate(parts, axis=0),
                ones,
                (((1,), (1,)), ((), ())),
                preferred_element_type=F32,
            )
        lines[block] = total[:128, :] + total[128:, :]
    waved = wide_by_data(x_table, jnp.concatenate([lines[b] for b in range(N_PATCH)], axis=1))
    lower = iota((128, 128), 1) < 64
    rows = []
    for z in range(4):
        tiles = []
        for t in range(4):
            start = 512 * t + 128 * (z // 2)
            even, odd = waved[:, start : start + 128], waved[:, start + 256 : start + 384]
            if z % 2 == 0:
                tiles.append(jnp.where(lower, even, pltpu.roll(odd, 64, 1)))
            else:
                tiles.append(jnp.where(lower, pltpu.roll(even, 64, 1), odd))
        rows.append(jnp.concatenate(tiles, axis=1))
    both = data_by_table(jnp.concatenate(rows, axis=0), y_table)
    kx = 8 * iota((64, 256), 0) + p
    first = iota((64, 256), 1) == 0
    alone = (kx == 0) | (kx == NX // 2)
    for z in range(4):
        real, imag = both[128 * z : 128 * z + 64], both[128 * z + 64 : 128 * z + 128]
        re_cos, re_sin = real[:, :256], real[:, 256:]
        im_cos, im_sin = imag[:, :256], imag[:, 256:]
        re_first = jnp.where(kx <= NX // 2, re_cos, re_sin)
        im_first = jnp.where(alone, re_sin, jnp.where(kx < NX // 2, im_cos, im_sin))
        out[:, z, :] = jnp.where(first, re_first, re_cos + im_sin)
        out[:, 4 + z, :] = jnp.where(first, im_first, im_cos - re_sin)


def spectrum_kernel(factor, kernel, lines, forward, backward, out):
    size = NY // 2
    green = kernel[0, :size, :].T
    base = factor[4]
    low, mid = kernel[0, 0:8, :].T[:, 0:1], kernel[0, size : size + 8, :].T[:, 0:1]
    first = iota((NZ, size), 1) == 0
    own = jnp.where(first, factor[0] * low + factor[1] * mid, base * green)
    mirrored = jnp.where(first[:, :128], factor[2] * low + factor[3] * mid, 0.0)
    value = lines[...].reshape(2 * NZ, size)
    sign = jnp.where((iota((2 * NZ, 128), 0) & 4) == 0, 1.0, -1.0)
    wave = table_by_data(forward, value)
    turned = table_by_data(forward, value[:, :128] * sign)
    left = jnp.concatenate([own[:, :128]] * 2, axis=0) * wave[:, :128]
    left = left + jnp.concatenate([mirrored] * 2, axis=0) * turned
    right = jnp.concatenate([own[:, 128:]] * 2, axis=0) * wave[:, 128:]
    scaled = jnp.concatenate([left, right], axis=1)
    out[...] = table_by_data(backward, scaled).reshape(N_SLAB, 8, size)


def gathered(whole, block, slot):
    row, low_col, cosine, sine = (jnp.broadcast_to(v, (8, 128)) for v in slot)
    row = row.astype(I32)
    low, upper = row & 127, row >= 128
    step = iota((8, 128), 0).astype(F32)
    total = jnp.zeros((8, 128), F32)
    for group in range(8):
        part = []
        for kind in range(2):
            at = slice(64 * kind + 8 * group, 64 * kind + 8 * group + 8)
            near = jnp.take_along_axis(whole[block, at, :128], low, axis=1, mode="promise_in_bounds")
            far = jnp.take_along_axis(whole[block, at, 128:], low, axis=1, mode="promise_in_bounds")
            part.append(jnp.where(upper, far, near))
        turned = part[0] * cosine - part[1] * sine
        total = total + jnp.where(low_col == step + 8.0 * group, turned, 0.0)
    return jnp.sum(total, axis=0, keepdims=True)


def backward_kernel(meta, arrived, data, quarter, x_table, y_table, out, slots, planes, blocks, whole):
    p = meta[0]
    for block in range(N_PATCH):
        row, low_col, cosine, sine = phases(data[block, 32:64, :], p, quarter)
        slots[0, block] = row
        slots[1, block] = low_col
        slots[2, block] = cosine
        slots[3, block] = sine
    value = arrived[...].reshape(512, 256)
    place = iota((512, 256), 0)
    real = (place & 4) == 0
    kx = 8 * (place >> 3) + p
    first = iota((512, 256), 1) == 0
    alone = (kx == 0) | (kx == NX // 2)
    after, before = pltpu.roll(value, 508, 0), pltpu.roll(value, 4, 0)
    keep = (kx <= NX // 2) & (real | ~alone)
    straight = jnp.where(first & ~keep, 0.0, value)
    other = jnp.where(kx > NX // 2, value, jnp.where(alone & real, after, 0.0))
    crossed = jnp.where(first, other, jnp.where(real, -after, before))
    planes[...] = data_by_table(jnp.concatenate([straight, crossed], axis=1), y_table).reshape(64, 8, 512)
    lower = iota((128, 128), 1) < 64
    both = [jnp.concatenate([planes[:, z, :], planes[:, 4 + z, :]], axis=0) for z in range(4)]
    waved = wide_by_data(x_table, jnp.concatenate(both, axis=1))
    for pair in range(2):
        for t in range(4):
            start = 1024 * pair + 128 * t
            even, odd = waved[:, start : start + 128], waved[:, start + 512 : start + 640]
            for block, tile in (
                (2 * t, jnp.where(lower, even, pltpu.roll(odd, 64, 1))),
                (2 * t + 1, jnp.where(lower, pltpu.roll(even, 64, 1), odd)),
            ):
                whole[block, :, 128 * pair : 128 * (pair + 1)] = tile
                high, low = split(tile)
                blocks[block, :128, 128 * pair : 128 * (pair + 1)] = high
                blocks[block, 128:, 128 * pair : 128 * (pair + 1)] = low

    steps = iota((64, 512), 0).astype(F32)

    for block in range(N_PATCH):
        field = blocks[block]
        for sender in range(N_PATCH):
            if sender in GATHERED:
                for q in range(4):
                    at = slice(8 * q + sender, 8 * q + sender + 1)
                    out[sender, 8 * q + block : 8 * q + block + 1, :] = gathered(
                        whole, block, [slots[k, block, at, :] for k in range(4)]
                    )
                continue
            in_row = one_hot(lanes(slots, block, sender, 0), 16, 256)
            ones = jnp.where(in_row, jnp.ones((256, 512), BF16), jnp.zeros((256, 512), BF16))
            near = mul(field, ones)
            re_part = near[0:64] + near[128:192]
            im_part = near[64:128] + near[192:256]
            turned = re_part * lanes(slots, block, sender, 2) - im_part * lanes(slots, block, sender, 3)
            in_col = lanes(slots, block, sender, 1) == steps
            found = jnp.sum(jnp.where(in_col, turned, 0.0), axis=0, keepdims=True)
            for q in range(4):
                out[sender, 8 * q + block : 8 * q + block + 1, :] = found[:, 128 * q : 128 * (q + 1)]


def sum_kernel(parts, out):
    total = parts[0]
    for p in range(1, N_PATCH):
        total = total + parts[p]
    out[:, 0, :] = unpaired(total).T


def near_kernel(data, index, coef, out):
    for j in range(4):
        at = slice(128 * j, 128 * (j + 1))
        total = jnp.zeros((8, 128), F32)
        for half in range(2):
            places = index[8 * half : 8 * half + 8, at]
            low, high = places & 127, places >> 7
            value = jnp.zeros(places.shape, F32)
            for h in range(32):
                value = jnp.where(high == h, lookup(data[h // 4, 64 + h % 4 : 65 + h % 4, :], low), value)
            total = total + coef[8 * half : 8 * half + 8, at] * value
        out[j : j + 1, :] = jnp.sum(total, axis=0, keepdims=True)


def interp_kernel(arrived, counts, panel, weight, near, out):
    used = iota((CAP, DEVICES), 0) < counts[...]
    thin = jnp.concatenate(thirds(arrived[:, 0, :].T), axis=1)
    expanded = mul(thin, jnp.concatenate([slab_of()] * 3, axis=0))
    keep = (iota((64, DEVICES), 1) & 7) == (iota((64, DEVICES), 0) & 7)
    expanded = jnp.where(keep, expanded, 0.0)
    rows = [jnp.sum(expanded[8 * c : 8 * c + 8, :], axis=0, keepdims=True) for c in range(CAP)]
    terms = jnp.where(used, weight[...] * jnp.concatenate(rows, axis=0), 0.0)
    places = panel[...]
    low, high = places & 127, places >> 7
    total = jnp.zeros((16, 128), F32)
    part = iota((16, DEVICES), 0)
    for c in range(CAP):
        term = terms[c : c + 1, :]
        top = term.astype(BF16).astype(F32)
        middle = (term - top).astype(BF16).astype(F32)
        bottom = term - top - middle
        shown = jnp.where(part < 4, top, jnp.where(part < 8, middle, jnp.where(part < 12, bottom, 0.0)))
        left = jnp.where((part & 3) == high[c : c + 1, :], shown, 0.0).astype(BF16)
        right = (iota((128, DEVICES), 0) == low[c : c + 1, :]).astype(F32).astype(BF16)
        total = total + lax.dot_general(left, right, (((1,), (1,)), ((), ())), preferred_element_type=F32)
    out[...] = total[0:4] + total[4:8] + total[8:12] + near[...]


VMEM = pl.BlockSpec(memory_space=pltpu.VMEM)
SMEM = pl.BlockSpec(memory_space=pltpu.SMEM)
FAR = pl.BlockSpec(memory_space=pltpu.HBM)


def call(kernel, shapes, args, scratch=(), scalars=0, vmem=16, sources=None, flops=10**7):
    many = isinstance(shapes, list)
    shape = [jax.ShapeDtypeStruct(s, F32) for s in (shapes if many else [shapes])]
    moved = 4 * sum(math.prod(o.shape) for o in shape) + sum(a.size * a.dtype.itemsize for a in args)
    return pl.pallas_call(
        kernel,
        out_shape=shape if many else shape[0],
        in_specs=sources or [SMEM] * scalars + [VMEM] * (len(args) - scalars),
        out_specs=[VMEM] * len(shape) if many else VMEM,
        scratch_shapes=list(scratch),
        compiler_params=pltpu.CompilerParams(vmem_limit_bytes=vmem * MIB),
        cost_estimate=pl.CostEstimate(flops=flops, bytes_accessed=moved, transcendentals=0),
    )(*args)


def call_far(kernel, shape, args):
    held = [pltpu.VMEM(a.shape, a.dtype) for a in args]
    done = [pltpu.SemaphoreType.DMA((len(args),))]
    return call(kernel, shape, args, held + done, vmem=60, sources=[FAR] * len(args))


def run_items(density, counts, panel, weight):
    return call_far(items_kernel, (N_SLAB, 1, 64), [density, counts, panel, weight])


def run_cells(density, row, col):
    return call(cells_kernel, (40, 128), [density, row, col], flops=10**9)


def run_message(arrived, cells):
    return call(message_kernel, (N_PATCH, 72, 128), [arrived, cells], flops=10**9)


def run_sum(parts):
    return call(sum_kernel, (N_SLAB, 1, 64), [parts])


def run_near(data, index, coef):
    return call(near_kernel, (4, 128), [data, index, coef])


def run_interp(*args):
    return call(interp_kernel, (4, 128), list(args))


def exchange(value, axis):
    return lax.all_to_all(value, axis, split_axis=0, concat_axis=0, tiled=True)


def run_forward(meta, data, quarter, x_table, y_table):
    return call(
        forward_kernel,
        (N_SLAB, 8, 256),
        [meta, data, quarter, x_table, y_table],
        [pltpu.VMEM((5, N_PATCH, 32, 128), F32), pltpu.VMEM((N_PATCH, 128, 256), F32)],
        scalars=1,
        vmem=32,
        flops=6 * 10**9,
    )


def run_spectrum(factor, kernel, lines, forward, backward):
    return call(
        spectrum_kernel, (N_SLAB, 8, 256), [factor, kernel, lines, forward, backward], scalars=1, vmem=24, flops=10**9
    )


def run_backward(meta, lines, data, quarter, x_table, y_table):
    return call(
        backward_kernel,
        (N_PATCH, 32, 128),
        [meta, lines, data, quarter, x_table, y_table],
        [
            pltpu.VMEM((4, N_PATCH, 32, 128), F32),
            pltpu.VMEM((N_SLAB, 8, 512), F32),
            pltpu.VMEM((N_PATCH, 256, 256), BF16),
            pltpu.VMEM((N_PATCH, 128, 256), F32),
        ],
        scalars=1,
        vmem=32,
        flops=6 * 10**9,
    )


def per_device(
    density,
    counts,
    send_panel,
    send_weight,
    interp_weight,
    recv_row,
    recv_col,
    kernel,
    near_index,
    near_coef,
):
    p = lax.axis_index("patch").astype(I32)
    own = lax.axis_index("slab").astype(I32) * N_PATCH + p
    meta = jnp.stack([p, own])
    quarter = jnp.asarray(quarter_table())
    x_forward, x_backward = (jnp.asarray(t) for t in x_tables())
    y_forward, y_backward = (jnp.asarray(t) for t in y_tables())
    z_forward, z_backward = (jnp.asarray(t) for t in z_tables())
    charge = density.reshape(4, 128)
    panel, weight, back_weight, row, col = (
        jnp.transpose(a[0]) for a in (send_panel, send_weight, interp_weight, recv_row, recv_col)
    )

    unit = 2.0 / (NX * NY * NZ)
    alone = (own == 0) | (own == NX // 2)
    below = own < NX // 2
    factor = jnp.stack(
        [
            jnp.where(alone, 0.25 * unit, jnp.where(below, unit, 0.0)),
            jnp.where(alone, 0.25 * unit, jnp.where(below, 0.0, unit)),
            jnp.where(alone, 0.25 * unit, 0.0),
            jnp.where(alone, -0.25 * unit, 0.0),
            jnp.full((), unit, F32),
        ]
    ).astype(F32)

    items = exchange(run_items(charge, counts, panel, weight), "slab")
    message = run_message(items, run_cells(charge, row, col))
    data = exchange(message, "patch")
    near = run_near(data, near_index, near_coef)

    lines = run_forward(meta, data, quarter, x_forward, y_forward)
    lines = exchange(lines, "slab")

    lines = run_spectrum(factor, kernel, lines, z_forward, z_backward)
    lines = exchange(lines, "slab")
    parts = run_backward(meta, lines, data, quarter, x_backward, y_backward)
    parts = exchange(parts, "patch")
    sampled = run_sum(parts)
    sampled = exchange(sampled, "slab")
    result = run_interp(sampled, counts, panel, back_weight, near)
    return result.reshape(-1)


def solution(mesh):
    placed = (
        P(("slab", "patch")),
        P(("slab", "patch"), None),
        P(("slab", "patch"), None, None),
        P(("slab", "patch"), None, None),
        P(("slab", "patch"), None, None),
        P(("slab", "patch"), None, None),
        P(("slab", "patch"), None, None),
        P(("slab", "patch"), None, None),
        P(None, ("slab", "patch")),
        P(None, ("slab", "patch")),
    )
    return jax.shard_map(
        per_device, mesh=mesh, in_specs=placed, out_specs=P(("slab", "patch")), check_vma=False
    )
```

```python
import math

import jax
import jax.numpy as jnp
import ml_dtypes
import numpy as np
from jax import lax
from jax.experimental import pallas as pl
from jax.experimental.pallas import tpu as pltpu
from jax.sharding import PartitionSpec as P

NX, NY, NZ = 512, 512, 256
N_SLAB, N_PATCH, CAP = 64, 8, 8
DEVICES = N_SLAB * N_PATCH
F32, BF16, I32 = jnp.float32, jnp.bfloat16, jnp.int32
MIB = 1024 * 1024
GATHERED = (0, 4)


def halves(table):
    high = table.astype(np.float32).astype(ml_dtypes.bfloat16)
    low = (table - high.astype(np.float64)).astype(np.float32).astype(ml_dtypes.bfloat16)
    return np.stack([high, low])


def wide(table):
    high, low = halves(table)
    return np.concatenate([high, high, low], axis=1)


def waves(first, second, length):
    turns = np.outer(first, second) % length
    angles = turns * (2.0 * np.pi / length)
    cosine, sine = np.cos(angles), np.sin(angles)
    cosine[(4 * turns == length) | (4 * turns == 3 * length)] = 0.0
    sine[(turns == 0) | (2 * turns == length)] = 0.0
    return cosine, sine


def x_tables():
    cosine, sine = waves(np.arange(64), np.arange(64), 64)
    forward = np.block([[cosine, sine], [-sine, cosine]])
    backward = np.block([[cosine, -sine], [sine, cosine]])
    return wide(forward), wide(backward)


def y_tables():
    cosine, sine = waves(np.arange(NY), np.arange(NY // 2), NY)
    sine[:, 0] = 1.0 - 2.0 * (np.arange(NY) % 2)
    return halves(np.concatenate([cosine, sine], axis=1)), halves(np.concatenate([cosine.T, sine.T], axis=0))


def z_tables():
    cosine, sine = waves(np.arange(NZ), np.arange(NZ), NZ)
    depth = NZ // N_SLAB

    def rows(re_part, im_part):
        parts = np.stack([re_part.reshape(N_SLAB, depth, -1), im_part.reshape(N_SLAB, depth, -1)], axis=1)
        return parts.reshape(2 * NZ, -1)

    forward = np.concatenate([rows(cosine, sine), rows(-sine, cosine)], axis=1).T
    backward = np.concatenate([rows(cosine, sine), rows(-sine, cosine)], axis=1)
    return halves(forward), halves(backward)


def quarter_table():
    cosine, sine = waves(np.arange(128), np.ones(1, np.int64), NX)
    return np.stack([cosine[:, 0], sine[:, 0]]).astype(np.float32)


def split(value):
    high = value.astype(BF16)
    return high, (value - high.astype(F32)).astype(BF16)


def mul(a, b):
    return jnp.dot(a, b, preferred_element_type=F32)


def data_by_table(value, table_ref):
    high, low = split(value)
    return mul(high, table_ref[0]) + mul(low, table_ref[0]) + mul(high, table_ref[1])


def table_by_data(table_ref, value):
    high, low = split(value)
    return mul(table_ref[0], high) + mul(table_ref[0], low) + mul(table_ref[1], high)


def wide_by_data(table_ref, value):
    high, low = split(value)
    return mul(table_ref[...], jnp.concatenate([high, low, high], axis=0))


def thirds(value):
    top = value.astype(BF16)
    rest = value - top.astype(F32)
    middle = rest.astype(BF16)
    return [top, middle, (rest - middle.astype(F32)).astype(BF16)]


def across(a, b):
    return lax.dot_general(a, b, (((1,), (1,)), ((), ())), preferred_element_type=F32)


def iota(shape, dim):
    return lax.broadcasted_iota(I32, shape, dim)


def spread(values):
    keep = (iota((8, DEVICES), 1) & 7) == iota((8, DEVICES), 0)
    rows = [jnp.where(keep, jnp.broadcast_to(values[c : c + 1, :], (8, DEVICES)), 0.0) for c in range(CAP)]
    return jnp.concatenate(rows, axis=0)


def slab_of():
    return ((iota((N_SLAB, DEVICES), 1) >> 3) == iota((N_SLAB, DEVICES), 0)).astype(F32).astype(BF16)


def paired(values):
    rows = [
        jnp.concatenate([values[16 * q : 16 * q + 8, :], values[16 * q + 8 : 16 * q + 16, :]], axis=1)
        for q in range(CAP // 2)
    ]
    return jnp.concatenate(rows, axis=0)


def unpaired(values):
    rows = []
    for q in range(CAP // 2):
        rows.append(values[8 * q : 8 * q + 8, :64])
        rows.append(values[8 * q : 8 * q + 8, 64:])
    return jnp.concatenate(rows, axis=0)


def lookup(row, places):
    return jnp.take_along_axis(
        jnp.broadcast_to(row, places.shape), places, axis=1, mode="promise_in_bounds"
    )


def fetch(sources, held, done):
    copies = [pltpu.make_async_copy(a, b, done.at[k]) for k, (a, b) in enumerate(zip(sources, held))]
    for copy in copies:
        copy.start()
    for copy in copies:
        copy.wait()


def items_kernel(*refs):
    sources, out, held, done = refs[:4], refs[4], refs[5:9], refs[9]
    slab = slab_of()
    fetch(sources, held, done)
    density, counts, panel, weight = held
    used = iota((CAP, DEVICES), 0) < counts[...]
    picked = []
    for j in range(4):
        places = panel[:, 128 * j : 128 * (j + 1)]
        low, high = places & 127, places >> 7
        value = jnp.zeros(places.shape, F32)
        for h in range(4):
            value = jnp.where(high == h, lookup(density[h : h + 1, :], low), value)
        picked.append(value)
    items = jnp.where(used, weight[...] * jnp.concatenate(picked, axis=1), 0.0)
    parts = across(slab, jnp.concatenate(thirds(spread(items)), axis=0))
    out[:, 0, :] = parts[:, :64] + parts[:, 64:128] + parts[:, 128:]


def cells_kernel(density, row, col, out):
    place = (row[...] * NX + col[...]).astype(F32)
    parts = across(jnp.concatenate(thirds(spread(place)), axis=0), slab_of())
    out[0:32, :] = paired(parts[:64] + parts[64:128] + parts[128:])
    out[32:36, :] = density[...]
    out[36:40, :] = density[...]


def message_kernel(arrived, cells, out):
    items = paired(arrived[:, 0, :].T)
    for p in range(N_PATCH):
        out[p, 0:32, :] = items
        out[p, 32:72, :] = cells[...]


def phases(cell, p, quarter):
    place = (cell + 0.5).astype(I32)
    col = place & (NX - 1)
    turn = (col * p) & (NX - 1)
    part, within = turn >> 7, turn & 127
    cosine, sine = lookup(quarter[0:1, :], within), lookup(quarter[1:2, :], within)
    odd = (part & 1) == 1
    real, imag = jnp.where(odd, sine, cosine), jnp.where(odd, cosine, sine)
    real = jnp.where((part == 1) | (part == 2), -real, real)
    imag = jnp.where(part >= 2, -imag, imag)
    return (place >> 9).astype(F32), (col & 63).astype(F32), real, imag


def lanes(ref, block, p, kind=0):
    rows = [ref[kind, block, 8 * q + p : 8 * q + p + 1, :] for q in range(4)]
    return jnp.concatenate(rows, axis=1)


def thick(row, count):
    return jnp.concatenate([jnp.broadcast_to(row, (16, row.shape[1])).astype(BF16)] * count, axis=0)


def one_hot(row, count, size):
    steps = lax.broadcasted_iota(I32, (size, row.shape[1]), 0).astype(F32).astype(BF16)
    return thick(row, count) == steps


def forward_kernel(meta, data, quarter, x_table, y_table, out, slots, lines):
    p = meta[0]
    for q in range(4):
        for sender in range(N_PATCH):
            slots[4, :, 8 * q + sender, :] = data[sender, 8 * q : 8 * q + 8, :]
    for block in range(N_PATCH):
        row, low_col, cosine, sine = phases(data[block, 32:64, :], p, quarter)
        slots[0, block] = row
        slots[1, block] = low_col
        slots[2, block] = slots[4, block] * cosine
        slots[3, block] = -slots[4, block] * sine

    for block in range(N_PATCH):
        total = jnp.zeros((256, 256), F32)
        for sender in range(N_PATCH):
            in_row = one_hot(lanes(slots, block, sender, 0), 16, 256)
            in_col = one_hot(lanes(slots, block, sender, 1), 4, 64)
            none = jnp.zeros((64, 512), BF16)
            re_high, re_low = split(lanes(slots, block, sender, 2))
            im_high, im_low = split(lanes(slots, block, sender, 3))
            parts = [jnp.where(in_col, thick(v.astype(F32), 4), none) for v in (re_high, im_high, re_low, im_low)]
            ones = jnp.where(in_row, jnp.ones((256, 512), BF16), jnp.zeros((256, 512), BF16))
            total = total + lax.dot_general(
                jnp.concatenate(parts, axis=0),
                ones,
                (((1,), (1,)), ((), ())),
                preferred_element_type=F32,
            )
        lines[block] = total[:128, :] + total[128:, :]
    waved = wide_by_data(x_table, jnp.concatenate([lines[b] for b in range(N_PATCH)], axis=1))
    lower = iota((128, 128), 1) < 64
    rows = []
    for z in range(4):
        tiles = []
        for t in range(4):
            start = 512 * t + 128 * (z // 2)
            even, odd = waved[:, start : start + 128], waved[:, start + 256 : start + 384]
            if z % 2 == 0:
                tiles.append(jnp.where(lower, even, pltpu.roll(odd, 64, 1)))
            else:
                tiles.append(jnp.where(lower, pltpu.roll(even, 64, 1), odd))
        rows.append(jnp.concatenate(tiles, axis=1))
    both = data_by_table(jnp.concatenate(rows, axis=0), y_table)
    kx = 8 * iota((64, 256), 0) + p
    first = iota((64, 256), 1) == 0
    alone = (kx == 0) | (kx == NX // 2)
    for z in range(4):
        real, imag = both[128 * z : 128 * z + 64], both[128 * z + 64 : 128 * z + 128]
        re_cos, re_sin = real[:, :256], real[:, 256:]
        im_cos, im_sin = imag[:, :256], imag[:, 256:]
        re_first = jnp.where(kx <= NX // 2, re_cos, re_sin)
        im_first = jnp.where(alone, re_sin, jnp.where(kx < NX // 2, im_cos, im_sin))
        out[:, z, :] = jnp.where(first, re_first, re_cos + im_sin)
        out[:, 4 + z, :] = jnp.where(first, im_first, im_cos - re_sin)


def spectrum_kernel(factor, kernel, lines, forward, backward, out, scaled):
    size = NY // 2
    green = kernel[0, :size, :].T
    base = factor[4]
    low, mid = kernel[0, 0:8, :].T[:, 0:1], kernel[0, size : size + 8, :].T[:, 0:1]
    first = iota((NZ, size), 1) == 0
    own = jnp.where(first, factor[0] * low + factor[1] * mid, base * green)
    mirrored = jnp.where(first[:, :128], factor[2] * low + factor[3] * mid, 0.0)
    value = lines[...].reshape(2 * NZ, size)
    sign = jnp.where((iota((2 * NZ, 128), 0) & 4) == 0, 1.0, -1.0)
    wave = table_by_data(forward, value)
    scaled[...] = jnp.concatenate([own] * 2, axis=0) * wave

    @pl.when(factor[2] > 0.0)
    def _():
        turned = table_by_data(forward, value[:, :128] * sign)
        scaled[:, :128] = scaled[:, :128] + jnp.concatenate([mirrored] * 2, axis=0) * turned

    out[...] = table_by_data(backward, scaled[...]).reshape(N_SLAB, 8, size)


def gathered(whole, block, slot):
    row, low_col, cosine, sine = (jnp.broadcast_to(v, (8, 128)) for v in slot)
    row = row.astype(I32)
    low, upper = row & 127, row >= 128
    step = iota((8, 128), 0).astype(F32)
    total = jnp.zeros((8, 128), F32)
    for group in range(8):
        part = []
        for kind in range(2):
            at = slice(64 * kind + 8 * group, 64 * kind + 8 * group + 8)
            near = jnp.take_along_axis(whole[block, at, :128], low, axis=1, mode="promise_in_bounds")
            far = jnp.take_along_axis(whole[block, at, 128:], low, axis=1, mode="promise_in_bounds")
            part.append(jnp.where(upper, far, near))
        turned = part[0] * cosine - part[1] * sine
        total = total + jnp.where(low_col == step + 8.0 * group, turned, 0.0)
    return jnp.sum(total, axis=0, keepdims=True)


def backward_kernel(meta, arrived, data, quarter, x_table, y_table, out, slots, planes, blocks, whole):
    p = meta[0]
    for block in range(N_PATCH):
        row, low_col, cosine, sine = phases(data[block, 32:64, :], p, quarter)
        slots[0, block] = row
        slots[1, block] = low_col
        slots[2, block] = cosine
        slots[3, block] = sine
    value = arrived[...].reshape(512, 256)
    place = iota((512, 256), 0)
    real = (place & 4) == 0
    kx = 8 * (place >> 3) + p
    first = iota((512, 256), 1) == 0
    alone = (kx == 0) | (kx == NX // 2)
    after, before = pltpu.roll(value, 508, 0), pltpu.roll(value, 4, 0)
    keep = (kx <= NX // 2) & (real | ~alone)
    straight = jnp.where(first & ~keep, 0.0, value)
    other = jnp.where(kx > NX // 2, value, jnp.where(alone & real, after, 0.0))
    crossed = jnp.where(first, other, jnp.where(real, -after, before))
    planes[...] = data_by_table(jnp.concatenate([straight, crossed], axis=1), y_table).reshape(64, 8, 512)
    lower = iota((128, 128), 1) < 64
    both = [jnp.concatenate([planes[:, z, :], planes[:, 4 + z, :]], axis=0) for z in range(4)]
    waved = wide_by_data(x_table, jnp.concatenate(both, axis=1))
    for pair in range(2):
        for t in range(4):
            start = 1024 * pair + 128 * t
            even, odd = waved[:, start : start + 128], waved[:, start + 512 : start + 640]
            for block, tile in (
                (2 * t, jnp.where(lower, even, pltpu.roll(odd, 64, 1))),
                (2 * t + 1, jnp.where(lower, pltpu.roll(even, 64, 1), odd)),
            ):
                whole[block, :, 128 * pair : 128 * (pair + 1)] = tile
                high, low = split(tile)
                blocks[block, :128, 128 * pair : 128 * (pair + 1)] = high
                blocks[block, 128:, 128 * pair : 128 * (pair + 1)] = low

    steps = iota((64, 512), 0).astype(F32)

    for block in range(N_PATCH):
        field = blocks[block]
        for sender in range(N_PATCH):
            if sender in GATHERED:
                for q in range(4):
                    at = slice(8 * q + sender, 8 * q + sender + 1)
                    out[sender, 8 * q + block : 8 * q + block + 1, :] = gathered(
                        whole, block, [slots[k, block, at, :] for k in range(4)]
                    )
                continue
            in_row = one_hot(lanes(slots, block, sender, 0), 16, 256)
            ones = jnp.where(in_row, jnp.ones((256, 512), BF16), jnp.zeros((256, 512), BF16))
            near = mul(field, ones)
            re_part = near[0:64] + near[128:192]
            im_part = near[64:128] + near[192:256]
            turned = re_part * lanes(slots, block, sender, 2) - im_part * lanes(slots, block, sender, 3)
            in_col = lanes(slots, block, sender, 1) == steps
            found = jnp.sum(jnp.where(in_col, turned, 0.0), axis=0, keepdims=True)
            for q in range(4):
                out[sender, 8 * q + block : 8 * q + block + 1, :] = found[:, 128 * q : 128 * (q + 1)]


def sum_kernel(parts, out):
    total = parts[0]
    for p in range(1, N_PATCH):
        total = total + parts[p]
    out[:, 0, :] = unpaired(total).T


def near_kernel(data, index, coef, out):
    for j in range(4):
        at = slice(128 * j, 128 * (j + 1))
        total = jnp.zeros((8, 128), F32)
        for half in range(2):
            places = index[8 * half : 8 * half + 8, at]
            low, high = places & 127, places >> 7
            value = jnp.zeros(places.shape, F32)
            for h in range(32):
                value = jnp.where(high == h, lookup(data[h // 4, 64 + h % 4 : 65 + h % 4, :], low), value)
            total = total + coef[8 * half : 8 * half + 8, at] * value
        out[j : j + 1, :] = jnp.sum(total, axis=0, keepdims=True)


def interp_kernel(arrived, counts, panel, weight, near, out):
    used = iota((CAP, DEVICES), 0) < counts[...]
    thin = jnp.concatenate(thirds(arrived[:, 0, :].T), axis=1)
    expanded = mul(thin, jnp.concatenate([slab_of()] * 3, axis=0))
    keep = (iota((64, DEVICES), 1) & 7) == (iota((64, DEVICES), 0) & 7)
    expanded = jnp.where(keep, expanded, 0.0)
    rows = [jnp.sum(expanded[8 * c : 8 * c + 8, :], axis=0, keepdims=True) for c in range(CAP)]
    terms = jnp.where(used, weight[...] * jnp.concatenate(rows, axis=0), 0.0)
    places = panel[...]
    low, high = places & 127, places >> 7
    total = jnp.zeros((16, 128), F32)
    part = iota((16, DEVICES), 0)
    for c in range(CAP):
        term = terms[c : c + 1, :]
        top = term.astype(BF16).astype(F32)
        middle = (term - top).astype(BF16).astype(F32)
        bottom = term - top - middle
        shown = jnp.where(part < 4, top, jnp.where(part < 8, middle, jnp.where(part < 12, bottom, 0.0)))
        left = jnp.where((part & 3) == high[c : c + 1, :], shown, 0.0).astype(BF16)
        right = (iota((128, DEVICES), 0) == low[c : c + 1, :]).astype(F32).astype(BF16)
        total = total + lax.dot_general(left, right, (((1,), (1,)), ((), ())), preferred_element_type=F32)
    out[...] = total[0:4] + total[4:8] + total[8:12] + near[...]


VMEM = pl.BlockSpec(memory_space=pltpu.VMEM)
SMEM = pl.BlockSpec(memory_space=pltpu.SMEM)
FAR = pl.BlockSpec(memory_space=pltpu.HBM)


def call(kernel, shapes, args, scratch=(), scalars=0, vmem=16, sources=None, flops=10**7):
    many = isinstance(shapes, list)
    shape = [jax.ShapeDtypeStruct(s, F32) for s in (shapes if many else [shapes])]
    moved = 4 * sum(math.prod(o.shape) for o in shape) + sum(a.size * a.dtype.itemsize for a in args)
    return pl.pallas_call(
        kernel,
        out_shape=shape if many else shape[0],
        in_specs=sources or [SMEM] * scalars + [VMEM] * (len(args) - scalars),
        out_specs=[VMEM] * len(shape) if many else VMEM,
        scratch_shapes=list(scratch),
        compiler_params=pltpu.CompilerParams(vmem_limit_bytes=vmem * MIB),
        cost_estimate=pl.CostEstimate(flops=flops, bytes_accessed=moved, transcendentals=0),
    )(*args)


def call_far(kernel, shape, args):
    held = [pltpu.VMEM(a.shape, a.dtype) for a in args]
    done = [pltpu.SemaphoreType.DMA((len(args),))]
    return call(kernel, shape, args, held + done, vmem=60, sources=[FAR] * len(args))


def run_items(density, counts, panel, weight):
    return call_far(items_kernel, (N_SLAB, 1, 64), [density, counts, panel, weight])


def run_cells(density, row, col):
    return call(cells_kernel, (40, 128), [density, row, col], flops=10**9)


def run_message(arrived, cells):
    return call(message_kernel, (N_PATCH, 72, 128), [arrived, cells], flops=10**9)


def run_sum(parts):
    return call(sum_kernel, (N_SLAB, 1, 64), [parts])


def run_near(data, index, coef):
    return call(near_kernel, (4, 128), [data, index, coef])


def run_interp(*args):
    return call(interp_kernel, (4, 128), list(args))


def exchange(value, axis):
    return lax.all_to_all(value, axis, split_axis=0, concat_axis=0, tiled=True)


def run_forward(meta, data, quarter, x_table, y_table):
    return call(
        forward_kernel,
        (N_SLAB, 8, 256),
        [meta, data, quarter, x_table, y_table],
        [pltpu.VMEM((5, N_PATCH, 32, 128), F32), pltpu.VMEM((N_PATCH, 128, 256), F32)],
        scalars=1,
        vmem=32,
        flops=6 * 10**9,
    )


def run_spectrum(factor, kernel, lines, forward, backward):
    return call(
        spectrum_kernel, (N_SLAB, 8, 256), [factor, kernel, lines, forward, backward],
        [pltpu.VMEM((2 * NZ, NY // 2), F32)], scalars=1, vmem=24, flops=10**9
    )


def run_backward(meta, lines, data, quarter, x_table, y_table):
    return call(
        backward_kernel,
        (N_PATCH, 32, 128),
        [meta, lines, data, quarter, x_table, y_table],
        [
            pltpu.VMEM((4, N_PATCH, 32, 128), F32),
            pltpu.VMEM((N_SLAB, 8, 512), F32),
            pltpu.VMEM((N_PATCH, 256, 256), BF16),
            pltpu.VMEM((N_PATCH, 128, 256), F32),
        ],
        scalars=1,
        vmem=32,
        flops=6 * 10**9,
    )


def per_device(
    density,
    counts,
    send_panel,
    send_weight,
    interp_weight,
    recv_row,
    recv_col,
    kernel,
    near_index,
    near_coef,
):
    p = lax.axis_index("patch").astype(I32)
    own = lax.axis_index("slab").astype(I32) * N_PATCH + p
    meta = jnp.stack([p, own])
    quarter = jnp.asarray(quarter_table())
    x_forward, x_backward = (jnp.asarray(t) for t in x_tables())
    y_forward, y_backward = (jnp.asarray(t) for t in y_tables())
    z_forward, z_backward = (jnp.asarray(t) for t in z_tables())
    charge = density.reshape(4, 128)
    panel, weight, back_weight, row, col = (
        jnp.transpose(a[0]) for a in (send_panel, send_weight, interp_weight, recv_row, recv_col)
    )

    unit = 2.0 / (NX * NY * NZ)
    alone = (own == 0) | (own == NX // 2)
    below = own < NX // 2
    factor = jnp.stack(
        [
            jnp.where(alone, 0.25 * unit, jnp.where(below, unit, 0.0)),
            jnp.where(alone, 0.25 * unit, jnp.where(below, 0.0, unit)),
            jnp.where(alone, 0.25 * unit, 0.0),
            jnp.where(alone, -0.25 * unit, 0.0),
            jnp.full((), unit, F32),
        ]
    ).astype(F32)

    items = exchange(run_items(charge, counts, panel, weight), "slab")
    message = run_message(items, run_cells(charge, row, col))
    data = exchange(message, "patch")
    near = run_near(data, near_index, near_coef)

    lines = run_forward(meta, data, quarter, x_forward, y_forward)
    lines = exchange(lines, "slab")

    lines = run_spectrum(factor, kernel, lines, z_forward, z_backward)
    lines = exchange(lines, "slab")
    parts = run_backward(meta, lines, data, quarter, x_backward, y_backward)
    parts = exchange(parts, "patch")
    sampled = run_sum(parts)
    sampled = exchange(sampled, "slab")
    result = run_interp(sampled, counts, panel, back_weight, near)
    return result.reshape(-1)


def solution(mesh):
    placed = (
        P(("slab", "patch")),
        P(("slab", "patch"), None),
        P(("slab", "patch"), None, None),
        P(("slab", "patch"), None, None),
        P(("slab", "patch"), None, None),
        P(("slab", "patch"), None, None),
        P(("slab", "patch"), None, None),
        P(("slab", "patch"), None, None),
        P(None, ("slab", "patch")),
        P(None, ("slab", "patch")),
    )
    return jax.shard_map(
        per_device, mesh=mesh, in_specs=placed, out_specs=P(("slab", "patch")), check_vma=False
    )
```
